128 devices in a mesh: tok: 2 (over core), hid: 16 (over y, x), ffn: 4 (over z).
Axes of the slice: x: 4, y: 4, z: 4, core: 2. Of those that a mesh axis runs over, the one named last changes fastest.
Arguments:
- inputs: bfloat16 [1536, 8192], P(('tok', 'ffn'), 'hid'), may hold values from -800 to 800
- cotangent: bfloat16 [1536, 8192], P(('tok', 'ffn'), 'hid'), may hold values from -0.59765625 to 0.59765625
- modality: int32 [1536], P('tok'), may hold values from 0 to 1
- modality_norm_gain: float32 [2, 8192], P(None, 'hid'), may hold values from 0.25 to 6
- modality_norm_bias: float32 [2, 8192], P(None, 'hid'), may hold values from -3 to 3
- w_gate: bfloat16 [8192, 11264], P(('hid', 'tok'), 'ffn'), may hold values from -0.0625 to 0.0625
- w_up: bfloat16 [8192, 11264], P(('hid', 'tok'), 'ffn'), may hold values from -0.0625 to 0.0625
- w_down: bfloat16 [11264, 8192], P('ffn', ('hid', 'tok')), may hold values from -0.0546875 to 0.0546875
Outputs:
- input_gradient: bfloat16 [1536, 8192], P(('tok', 'ffn'), 'hid')
- grad_gate: float32 [8192, 11264], P(('hid', 'tok'), 'ffn')
- grad_up: float32 [8192, 11264], P(('hid', 'tok'), 'ffn')
- grad_down: float32 [11264, 8192], P('ffn', ('hid', 'tok'))
- gain_gradient: float32 [2, 8192], P(None, 'hid')
- grad_bias: float32 [2, 8192], P(None, 'hid')
The draws below stay inside these ranges and needn't reach their ends.
All inputs are finite; a program needn't handle non-finite values.
Results may differ from the reference program's by a relative error of at most 0.025.
Values may be sent and summed in bfloat16 or wider, within the bound.
A program may use at most 128 MiB of HBM per device.

```python
import math
import jax
import jax.numpy as jnp
from jax import lax

MODEL_WIDTH = 8192
FF = 11264
MODES = 2
TOK_DEV = 768
TOKENS = 1536
N_TOK = 2
N_HID = 16


def feature_ramp(top):
    position = jnp.arange(MODEL_WIDTH, dtype=jnp.float32) / (MODEL_WIDTH - 1)
    return jnp.exp(position * math.log(top))


def draw_inputs(key, part):
    key = jax.random.fold_in(key, 7)
    first, second, third = jax.random.split(key, 3)
    rough = jnp.exp(jax.random.uniform(second, (1, MODEL_WIDTH), jnp.float32, 0.0, math.log(2.0)))
    base = jnp.clip(jax.random.normal(first, (TOKENS, MODEL_WIDTH), jnp.float32), -4.0, 4.0)
    column = feature_ramp(10.0)[None, :] * rough
    row_scale = jnp.exp(jax.random.uniform(third, (TOKENS, 1), jnp.float32, 0.0, math.log(10.0)))
    return (base * column * row_scale).astype(jnp.bfloat16)


def draw_modality_norm_gain(key, part):
    key = jax.random.fold_in(key, 11)
    rough = jnp.exp(jax.random.uniform(key, (MODES, MODEL_WIDTH), jnp.float32, math.log(0.75), math.log(1.33)))
    ramp = 0.5 * feature_ramp(6.0)
    return (ramp[None, :] * rough).astype(jnp.float32)


def set_ends(values, stream_key, smallest, largest):
    dims = values.shape
    place = [jax.random.randint(jax.random.fold_in(stream_key, axis), (), 0, dims[axis]) for axis in range(len(dims))]
    values = values.at[tuple(place)].set(smallest)
    longest = dims.index(max(dims))
    place[longest] = (place[longest] + 1) % dims[longest]
    return values.at[tuple(place)].set(largest)


def spiked(values, stream_key, source, target, parts, factor):
    owner, partner = [(jnp.arange(values.shape[dim]) // (values.shape[dim] // parts)).reshape([-1 if axis == dim else 1 for axis in range(values.ndim)]) for dim in (source, target)]
    chosen = jax.random.permutation(stream_key, parts)[partner]
    strong = (owner == chosen) | (owner == (partner + parts // 2) % parts)
    return jnp.where(strong, factor * values, values)


def levels(own_key, extent, pieces, low, top_value):
    def one(axis_at, parts):
        steps = jax.random.uniform(jax.random.fold_in(jax.random.fold_in(own_key, 6), axis_at), (parts,), jnp.float32, low / len(pieces), top_value / len(pieces))
        return jnp.repeat(jnp.exp(steps), extent[axis_at] // parts).reshape((-1,) + (1,) * (len(extent) - axis_at - 1))

    gain = one(*pieces[0])
    for cut in pieces[1:]:
        gain = gain * one(*cut)
    return gain


def centred(rng, dims, deviation, reach, cuts=(), kind=jnp.bfloat16):
    entries = deviation * jax.random.normal(rng, dims, jnp.float32)
    if cuts:
        entries = entries * levels(rng, dims, cuts, -0.22, 0.18)
    return jnp.clip(entries, -reach, reach).astype(kind)


def bell_draw_with(own_key, dims, scale, bound, cuts, heavy, held_as=jnp.bfloat16):
    result = scale * jax.random.normal(own_key, dims, jnp.float32)
    if cuts:
        result = result * levels(own_key, dims, cuts, -0.22, 0.18)
    return jnp.clip(spiked(result, jax.random.fold_in(own_key, 3), *heavy), -bound, bound).astype(held_as)


def setup_inputs(seed: int = 0) -> dict:
    arg_keys = jax.random.split(jax.random.key(seed), 9)
    inputs = draw_inputs(jax.random.fold_in(arg_keys[8], 71), 0)
    cotangent = bell_draw_with(arg_keys[1], (TOKENS, MODEL_WIDTH), 0.1, 0.59765625, ((0, 8), (1, 16)), (0, 1, 16, 2.0))
    modality = set_ends(jax.random.randint(arg_keys[2], (TOKENS,), 0, 2), jax.random.fold_in(arg_keys[2], 1), 0, 1).astype(jnp.int32)
    modality_norm_gain = draw_modality_norm_gain(jax.random.fold_in(arg_keys[8], 71), 0)
    modality_norm_bias = centred(arg_keys[4], (MODES, MODEL_WIDTH), 0.5, 3.0, ((1, 16),), jnp.float32)
    w_gate = centred(arg_keys[5], (MODEL_WIDTH, FF), MODEL_WIDTH ** -0.5, 0.0625, ((0, 32), (1, 4)))
    w_up = centred(arg_keys[6], (MODEL_WIDTH, FF), MODEL_WIDTH ** -0.5, 0.0625, ((0, 32), (1, 4)))
    w_down = centred(arg_keys[7], (FF, MODEL_WIDTH), FF ** -0.5, 0.0546875, ((0, 4), (1, 32)))
    return {"inputs": inputs, "cotangent": cotangent, "modality": modality, "modality_norm_gain": modality_norm_gain, "modality_norm_bias": modality_norm_bias, "w_gate": w_gate, "w_up": w_up, "w_down": w_down}


eps = 1e-05

def selected_rows(modality, table):
    return jnp.where(modality[:, None] == 1, table[1][None, :], table[0][None, :])

def rounded(value):
    return lax.optimization_barrier(value.astype(jnp.bfloat16)).astype(jnp.float32)

def reference(inputs, cotangent, modality, modality_norm_gain, modality_norm_bias, w_gate, w_up, w_down):
    value_entries = inputs.astype(jnp.float32)
    row_average = lax.optimization_barrier(jnp.sum(value_entries, -1)) / MODEL_WIDTH
    variance = lax.optimization_barrier(jnp.sum(value_entries * value_entries, -1)) / MODEL_WIDTH - row_average * row_average
    inverse_deviation = lax.rsqrt(variance + eps)
    centered_input = (value_entries - row_average[:, None]) * inverse_deviation[:, None]
    selected_gain = selected_rows(modality, modality_norm_gain)
    selected_bias = selected_rows(modality, modality_norm_bias)
    standardized_rows = (centered_input * selected_gain + selected_bias).astype(jnp.bfloat16)
    width = MODEL_WIDTH // N_HID
    gate = jnp.zeros((TOKENS, FF), jnp.float32)
    up = jnp.zeros((TOKENS, FF), jnp.float32)
    dact = jnp.zeros((TOKENS, FF), jnp.float32)
    for block in range(N_HID):
        first = block * width
        normed_b = standardized_rows[:, first:first + width]
        gate = gate + rounded(jnp.dot(normed_b, w_gate[first:first + width], preferred_element_type=jnp.float32))
        up = up + rounded(jnp.dot(normed_b, w_up[first:first + width], preferred_element_type=jnp.float32))
        dact = dact + rounded(jnp.dot(cotangent[:, first:first + width], w_down[:, first:first + width].T, preferred_element_type=jnp.float32))
    sigmoid_gate = jax.nn.sigmoid(gate)
    silu_gate = gate * sigmoid_gate
    act = (silu_gate * up).astype(jnp.bfloat16)
    dgate = (dact * up * sigmoid_gate * (1.0 + gate * (1.0 - sigmoid_gate))).astype(jnp.bfloat16)
    dup = (dact * silu_gate).astype(jnp.bfloat16)
    grad_gate = jnp.zeros((MODEL_WIDTH, FF), jnp.float32)
    grad_up = jnp.zeros((MODEL_WIDTH, FF), jnp.float32)
    grad_down = jnp.zeros((FF, MODEL_WIDTH), jnp.float32)
    for block in range(N_TOK):
        first = block * TOK_DEV
        normed_b = standardized_rows[first:first + TOK_DEV]
        part_gate = jnp.dot(normed_b.T, dgate[first:first + TOK_DEV], preferred_element_type=jnp.float32)
        part_up = jnp.dot(normed_b.T, dup[first:first + TOK_DEV], preferred_element_type=jnp.float32)
        part_down = jnp.dot(act[first:first + TOK_DEV].T, cotangent[first:first + TOK_DEV], preferred_element_type=jnp.float32)
        grad_gate = grad_gate + rounded(part_gate)
        grad_up = grad_up + rounded(part_up)
        grad_down = grad_down + rounded(part_down)
    normed_gradient = jnp.dot(dgate, w_gate.T, preferred_element_type=jnp.float32) + jnp.dot(dup, w_up.T, preferred_element_type=jnp.float32)
    centered_gradient = normed_gradient * selected_gain
    gradient_average = lax.optimization_barrier(jnp.sum(centered_gradient, -1)) / MODEL_WIDTH
    product_average = lax.optimization_barrier(jnp.sum(centered_gradient * centered_input, -1)) / MODEL_WIDTH
    input_gradient = (inverse_deviation[:, None] * (centered_gradient - gradient_average[:, None] - centered_input * product_average[:, None]) + cotangent.astype(jnp.float32)).astype(jnp.bfloat16)
    modality_indicator = (modality[:, None] == jnp.arange(2, dtype=jnp.int32)[None, :]).astype(jnp.float32)
    gain_gradient = jnp.dot(modality_indicator.T, normed_gradient * centered_input, precision=lax.Precision.HIGHEST)
    grad_bias = jnp.dot(modality_indicator.T, normed_gradient, precision=lax.Precision.HIGHEST)
    return (input_gradient, grad_gate, grad_up, grad_down, gain_gradient, grad_bias)
```

```python
import functools

import jax
import jax.numpy as jnp
from jax import lax
from jax.experimental import pallas as pl
from jax.experimental.pallas import tpu as pltpu
from jax.sharding import PartitionSpec as P

WIDTH = 8192
EPS = 1e-05
RING = 4
LANES = 128
CHUNK = 256
AHEAD = 3
MESH = pl.DeviceIdType.MESH
F32 = jnp.float32
BF16 = jnp.bfloat16


def dot_nn(a, b):
    return lax.dot_general(a, b, (((1,), (0,)), ((), ())), preferred_element_type=F32)


def dot_nt(a, b):
    return lax.dot_general(a, b, (((1,), (1,)), ((), ())), preferred_element_type=F32)


def dot_tn(a, b):
    return lax.dot_general(a, b, (((0,), (0,)), ((), ())), preferred_element_type=F32)


def block_kernel(
    n_chunks,
    x_ref, dy_ref, mod_ref, gain_ref, bias_ref, wg_hbm, wu_hbm, wd_hbm,
    ig_ref, gain_out, bias_out, gg_hbm, gu_hbm, gd_hbm,
    wg, wu, wd, dy, nrm, nrm_t, dn_acc, dn_send, dn_recv,
    pd, pg, rld, rlg, fmd, fmg, fpd, fpg, rld2, rlg2, fmd2, fmg2, fpd2, fpg2,
    gat, t_send, t_recv, o_stage,
    st_src, st_recv, gb_src, gb_recv,
    w_local, w_send, w_recv, z_send, z_recv, st_send, st_sem, gb_send, gb_sem,
    s1, s2, r1, r2, as1, as2, a1, a2, ts, tr, od,
):
    t = lax.axis_index("tok")
    h = lax.axis_index("hid")
    z = lax.axis_index("ffn")
    y = lax.div(h, RING)
    x = lax.rem(h, RING)
    rows, feats = x_ref.shape
    half = feats // 2
    sub = rows // RING

    def dev(axis, d):
        if axis == "x":
            return (t, y * RING + lax.rem(x + d, RING), z)
        if axis == "y":
            return (t, lax.rem(y + d, RING) * RING + x, z)
        if axis == "z":
            return (t, h, lax.rem(z + d, RING))
        return (1 - t, h, z)

    def send(src, dst, ssem, rsem, to):
        pltpu.make_async_remote_copy(
            src_ref=src, dst_ref=dst, send_sem=ssem, recv_sem=rsem, device_id=to, device_id_type=MESH
        ).start()

    def wait(ref, sem):
        pltpu.make_async_copy(ref, ref, sem).wait()

    barrier = pltpu.get_barrier_semaphore()
    for axis in ("x", "y", "z"):
        for d in (1, 2, 3):
            pl.semaphore_signal(barrier, inc=1, device_id=dev(axis, d), device_id_type=MESH)
    pl.semaphore_signal(barrier, inc=1, device_id=dev("c", 1), device_id_type=MESH)

    mine = pl.ds(pl.multiple_of(t * half, half), half)
    other = pl.ds(pl.multiple_of((1 - t) * half, half), half)
    zrows = pl.ds(pl.multiple_of(z * rows, rows), rows)
    w_pairs = ((wd_hbm, wd.at[t]), (wg_hbm, wg.at[mine]), (wu_hbm, wu.at[mine]))
    for k, (src, dst) in enumerate(w_pairs):
        pltpu.make_async_copy(src, dst, w_local.at[k]).start()
    dy[zrows] = dy_ref[...]
    dn_acc[...] = jnp.zeros_like(dn_acc)

    lane = lax.broadcasted_iota(jnp.int32, (rows, LANES), 1)

    def pack(a, b):
        both = jnp.where(lane == 0, a, jnp.where(lane == 1, b, 0.0))
        both = jnp.concatenate([both, jnp.zeros((256 - rows, LANES), F32)], axis=0)
        return both.T[0:8]

    def unpack(v):
        back = jnp.concatenate([v, jnp.zeros((LANES - 8, 256), F32)], axis=0).T
        return back[0:rows, 0:1], back[0:rows, 1:2]

    def stat_send(use, axis, k):
        for d in (1, 2, 3):
            send(st_src.at[use, k], st_recv.at[use, k, d - 1], st_send.at[use, k], st_sem.at[use, k, d - 1], dev(axis, d))

    def stat_take(use, k):
        total = st_src[use, k]
        for d in (1, 2, 3):
            wait(st_recv.at[use, k, d - 1], st_sem.at[use, k, d - 1])
            total = total + st_recv[use, k, d - 1]
        wait(st_recv.at[use, k], st_send.at[use, k])
        return total

    xv = x_ref[...].astype(F32)
    st_src[0, 0] = pack(jnp.sum(xv, -1, keepdims=True), jnp.sum(xv * xv, -1, keepdims=True))

    pl.semaphore_wait(barrier, 10)

    for d in (1, 3, 2):
        send(dy.at[zrows], dy.at[zrows], z_send.at[0], z_recv.at[0, d - 1], dev("z", d))
    stat_send(0, "x", 0)
    for k, (src, dst) in enumerate(w_pairs):
        send(src, dst, w_send.at[k], w_recv.at[k], dev("c", 1))

    def second_is_one():
        return mod_ref[...] == 1.0

    def gain_selected():
        return jnp.where(second_is_one()[:, 0:1], gain_ref[1:2], gain_ref[0:1])

    def moments(total):
        s, sq = unpack(total)
        mean = s / WIDTH
        return mean, lax.rsqrt(sq / WIDTH - mean * mean + EPS)

    def normalised():
        mean, inv = moments(st_src[0, 2])
        return (x_ref[...].astype(F32) - mean) * inv, inv

    def take_dy():
        for d in (1, 3, 2):
            wait(dy.at[zrows], z_recv.at[0, d - 1])
        wait(wd.at[t], w_local.at[0])
        wait(wd.at[t], w_recv.at[0])

    def stat_second():
        st_src[0, 1] = stat_take(0, 0)
        stat_send(0, "y", 1)

    def norm_send():
        st_src[0, 2] = stat_take(0, 1)
        xhat, _ = normalised()
        bias = jnp.where(second_is_one()[:, 0:1], bias_ref[1:2], bias_ref[0:1])
        nrm[zrows] = (xhat * gain_selected() + bias).astype(BF16)
        for d in (1, 3, 2):
            send(nrm.at[zrows], nrm.at[zrows], z_send.at[1], z_recv.at[1, d - 1], dev("z", d))

    def norm_take():
        for d in (1, 3, 2):
            wait(nrm.at[zrows], z_recv.at[1, d - 1])
        for k in (1, 2):
            wait(wg.at[mine], w_local.at[k])
            wait(wg.at[mine], w_recv.at[k])
        nrm_t[...] = nrm[...].T

    def columns(c):
        return pl.ds(pl.multiple_of(c * CHUNK, CHUNK), CHUNK)

    first = (("x", x, "y", y), ("y", y, "x", x))

    kinds = (
        dict(p=pd, rl=rld, fm=fmd, fp=fpd, rl2=rld2, fm2=fmd2, fp2=fpd2, cut=32, k=0),
        dict(p=pg, rl=rlg, fm=fmg, fp=fpg, rl2=rlg2, fm2=fmg2, fp2=fpg2, cut=48, k=1),
    )

    def ring(p):
        return lax.rem(p + 1, RING), lax.rem(p + 2, RING), lax.rem(p + 3, RING)

    def rs_send(kind, c):
        p, rl, fm, fp, k = kind["p"], kind["rl"], kind["fm"], kind["fp"], kind["k"]
        for o in (0, 1):
            ax, me, _, _ = first[o]
            nxt, opp, prv = ring(me)
            ss = s1.at[k, c, o]
            lo, hi = pl.ds(0, 2), pl.ds(2, 2)
            send(p.at[c, o, opp, lo], rl.at[c, o, lo], ss, r1.at[k, c, o, 0], dev(ax, 1))
            send(p.at[c, o, opp, hi], rl.at[c, o, hi], ss, r1.at[k, c, o, 1], dev(ax, 3))
            send(p.at[c, o, nxt, hi], fm.at[c, o, hi], ss, r1.at[k, c, o, 2], dev(ax, 1))
            send(p.at[c, o, prv, lo], fp.at[c, o, lo], ss, r1.at[k, c, o, 3], dev(ax, 3))

    def rs_relay(kind, c):
        p, rl, fm, fp, k = kind["p"], kind["rl"], kind["fm"], kind["fp"], kind["k"]
        for o in (0, 1):
            ax, me, _, _ = first[o]
            nxt, opp, prv = ring(me)
            ss = s1.at[k, c, o]
            for part, to, d, sem, buf, rsem in (
                (pl.ds(0, 2), nxt, 1, 0, fm, 2),
                (pl.ds(2, 2), prv, 3, 1, fp, 3),
            ):
                wait(rl.at[c, o, part], r1.at[k, c, o, sem])
                p[c, o, to, part] = p[c, o, to, part] + rl[c, o, part]
                send(p.at[c, o, to, part], buf.at[c, o, part], ss, r1.at[k, c, o, rsem], dev(ax, d))

    def rs_turn(kind, c):
        p, fm, fp, k = kind["p"], kind["fm"], kind["fp"], kind["k"]
        rl2, fm2, fp2, cut = kind["rl2"], kind["fm2"], kind["fp2"], kind["cut"]
        size = p.shape[4]
        for o in (0, 1):
            _, me, bx, me2 = first[o]
            wait(fm.at[c, o], r1.at[k, c, o, 2])
            wait(fp.at[c, o], r1.at[k, c, o, 3])
            p[c, o, me] = (p[c, o, me].astype(F32) + fm[c, o].astype(F32) + fp[c, o].astype(F32)).astype(BF16)
            nxt, opp, prv = ring(me2)
            ss = s2.at[k, c, o]
            lo, hi = pl.ds(0, cut), pl.ds(cut, size - cut)
            send(p.at[c, o, me, opp, lo], rl2.at[c, o, lo], ss, r2.at[k, c, o, 0], dev(bx, 1))
            send(p.at[c, o, me, opp, hi], rl2.at[c, o, hi], ss, r2.at[k, c, o, 1], dev(bx, 3))
            send(p.at[c, o, me, nxt, hi], fm2.at[c, o, hi], ss, r2.at[k, c, o, 2], dev(bx, 1))
            send(p.at[c, o, me, prv, lo], fp2.at[c, o, lo], ss, r2.at[k, c, o, 3], dev(bx, 3))

    def rs_relay2(kind, c):
        p, k, cut = kind["p"], kind["k"], kind["cut"]
        rl2, fm2, fp2 = kind["rl2"], kind["fm2"], kind["fp2"]
        size = p.shape[4]
        for o in (0, 1):
            _, me, bx, me2 = first[o]
            nxt, opp, prv = ring(me2)
            ss = s2.at[k, c, o]
            for part, to, d, sem, buf, rsem in (
                (pl.ds(0, cut), nxt, 1, 0, fm2, 2),
                (pl.ds(cut, size - cut), prv, 3, 1, fp2, 3),
            ):
                wait(rl2.at[c, o, part], r2.at[k, c, o, sem])
                p[c, o, me, to, part] = p[c, o, me, to, part] + rl2[c, o, part]
                send(p.at[c, o, me, to, part], buf.at[c, o, part], ss, r2.at[k, c, o, rsem], dev(bx, d))

    def rs_final(kind, c, o):
        p, k, fm2, fp2 = kind["p"], kind["k"], kind["fm2"], kind["fp2"]
        _, me, _, me2 = first[o]
        wait(fm2.at[c, o], r2.at[k, c, o, 2])
        wait(fp2.at[c, o], r2.at[k, c, o, 3])
        wait(p.at[c, o, pl.ds(0, 3)], s1.at[k, c, o])
        wait(p.at[c, o, 0, pl.ds(0, 3)], s2.at[k, c, o])
        return p[c, o, me, me2].astype(F32) + fm2[c, o].astype(F32) + fp2[c, o].astype(F32)

    def d_start(c):
        part = dot_nt(dy[:, 0:half], wd[0, columns(c)]) + dot_nt(dy[:, half:feats], wd[1, columns(c)])
        part = part.astype(BF16)
        for o in (0, 1):
            v = part[:, o * LANES:(o + 1) * LANES]
            for q in range(RING):
                for s in range(RING):
                    r = q * rows + s * sub
                    pd[c, o, q, s] = v[r:r + sub]
        rs_send(kinds[0], c)

    def g_start(c):
        for a, w in ((0, wg), (1, wu)):
            part = dot_nn(nrm[...], w[:, columns(c)]).astype(BF16)
            for o in (0, 1):
                v = part[:, o * LANES:(o + 1) * LANES]
                for q in range(RING):
                    for s in range(RING):
                        r = q * rows + s * sub
                        pg[c, o, q, s, a * sub:(a + 1) * sub] = v[r:r + sub]
        rs_send(kinds[1], c)

    def point(c):
        for o in (0, 1):
            _, me, bx, me2 = first[o]
            dact = rs_final(kinds[0], c, o)
            gu = rs_final(kinds[1], c, o)
            gate, up = gu[0:sub], gu[sub:2 * sub]
            sig = jax.nn.sigmoid(gate)
            silu = gate * sig
            gat[c, o, me, me2, 0:sub] = (silu * up).astype(BF16)
            gat[c, o, me, me2, sub:2 * sub] = (dact * up * sig * (1.0 + gate * (1.0 - sig))).astype(BF16)
            gat[c, o, me, me2, 2 * sub:3 * sub] = (dact * silu).astype(BF16)
            piece = gat.at[c, o, me, me2]
            send(piece, piece, as1.at[c, o], a1.at[c, o, 0], dev(bx, 1))
            send(piece, piece, as1.at[c, o], a1.at[c, o, 1], dev(bx, 3))

    def ag_relay(c):
        for o in (0, 1):
            _, me, bx, me2 = first[o]
            nxt, opp, prv = ring(me2)
            for part, frm, d, sem in ((pl.ds(0, 64), prv, 1, 0), (pl.ds(64, 3 * sub - 64), nxt, 3, 1)):
                wait(gat.at[c, o, me, frm], a1.at[c, o, sem])
                ref = gat.at[c, o, me, frm, part]
                send(ref, ref, as1.at[c, o], a1.at[c, o, 2], dev(bx, d))

    def ag_turn(c):
        for o in (0, 1):
            ax, me, _, me2 = first[o]
            _, opp, _ = ring(me2)
            wait(gat.at[c, o, me, opp], a1.at[c, o, 2])
            ref = gat.at[c, o, me]
            send(ref, ref, as2.at[c, o], a2.at[c, o, 0], dev(ax, 1))
            send(ref, ref, as2.at[c, o], a2.at[c, o, 1], dev(ax, 3))

    def ag_relay2(c):
        for o in (0, 1):
            ax, me, _, _ = first[o]
            nxt, opp, prv = ring(me)
            for part, frm, d, sem in ((pl.ds(0, 2), prv, 1, 0), (pl.ds(2, 2), nxt, 3, 1)):
                wait(gat.at[c, o, frm], a2.at[c, o, sem])
                ref = gat.at[c, o, frm, part]
                send(ref, ref, as2.at[c, o], a2.at[c, o, 2], dev(ax, d))

    def out_copies(c, slot):
        return (
            pltpu.make_async_copy(o_stage.at[slot, 0], gg_hbm.at[:, columns(c)], od.at[slot, 0]),
            pltpu.make_async_copy(o_stage.at[slot, 1], gu_hbm.at[:, columns(c)], od.at[slot, 1]),
            pltpu.make_async_copy(o_stage.at[slot, 2], gd_hbm.at[columns(c)], od.at[slot, 2]),
        )

    def grads(c):
        slot = lax.rem(c, 2)
        for o in (0, 1):
            _, me, _, _ = first[o]
            _, opp, _ = ring(me)
            wait(gat.at[c, o, opp], a2.at[c, o, 2])
            wait(gat.at[c, o, 0, pl.ds(0, 3)], as1.at[c, o])
            wait(gat.at[c, o, pl.ds(0, 3)], as2.at[c, o])

        def whole(a):
            return jnp.concatenate(
                [gat[c, o, :, :, a * sub:(a + 1) * sub].reshape(RING * rows, LANES) for o in (0, 1)], axis=1
            )

        act, dgate, dup = whole(0), whole(1), whole(2)
        t_send[slot, 0] = dot_nn(nrm_t[other], dgate).astype(BF16)
        t_send[slot, 1] = dot_nn(nrm_t[other], dup).astype(BF16)
        t_send[slot, 2] = dot_tn(act, dy[:, other]).astype(BF16)
        send(t_send.at[slot], t_recv.at[c], ts.at[slot], tr.at[c], dev("c", 1))

        @pl.when(c >= 2)
        def _():
            for copy in out_copies(c, slot):
                copy.wait()

        o_stage[slot, 0] = dot_nn(nrm_t[mine], dgate)
        o_stage[slot, 1] = dot_nn(nrm_t[mine], dup)
        o_stage[slot, 2] = dot_tn(act, dy[:, mine])
        dn_acc[...] += dot_nt(dgate, wg[:, columns(c)]) + dot_nt(dup, wu[:, columns(c)])

    def finish(c):
        slot = lax.rem(c, 2)
        wait(t_recv.at[c], tr.at[c])
        wait(t_send.at[slot], ts.at[slot])
        for k in range(3):
            o_stage[slot, k] = o_stage[slot, k] + t_recv[c, k].astype(F32)
        for copy in out_copies(c, slot):
            copy.start()

    take_dy()

    def tick(i, _):
        def at(off, step):
            c = i - off
            pl.when(jnp.logical_and(c >= 0, c < n_chunks))(lambda: step(c))

        at(AHEAD + 9, finish)
        at(AHEAD + 8, grads)
        at(AHEAD + 7, ag_relay2)
        at(AHEAD + 6, ag_turn)
        at(AHEAD + 5, ag_relay)
        at(AHEAD + 4, point)
        at(AHEAD + 3, functools.partial(rs_relay2, kinds[1]))
        at(3, functools.partial(rs_relay2, kinds[0]))
        at(AHEAD + 2, functools.partial(rs_turn, kinds[1]))
        at(2, functools.partial(rs_turn, kinds[0]))
        at(AHEAD + 1, functools.partial(rs_relay, kinds[1]))
        at(1, functools.partial(rs_relay, kinds[0]))
        pl.when(i == AHEAD)(norm_take)
        at(AHEAD, g_start)
        at(0, d_start)
        pl.when(i == 0)(stat_second)
        pl.when(i == 1)(norm_send)
        return 0

    lax.fori_loop(0, n_chunks + AHEAD + 10, tick, 0)

    dn_send[...] = dn_acc[...].astype(BF16)
    for d in (1, 3, 2):
        rows_to = pl.ds(pl.multiple_of(lax.rem(z + d, RING) * rows, rows), rows)
        send(dn_send.at[rows_to], dn_recv.at[d - 1], z_send.at[2], z_recv.at[2, d - 1], dev("z", d))
    for slot in (0, 1):
        for copy in out_copies(0, slot):
            copy.wait()
    xhat, inv = normalised()
    dn = dn_acc[zrows]
    for d in (1, 3, 2):
        wait(dn_recv.at[d - 1], z_recv.at[2, d - 1])
        dn = dn + dn_recv[d - 1].astype(F32)
    dxhat = dn * gain_selected()
    st_src[1, 0] = pack(jnp.sum(dxhat, -1, keepdims=True), jnp.sum(dxhat * xhat, -1, keepdims=True))
    stat_send(1, "x", 0)
    ind = mod_ref[:, 0:1]
    dnx = dn * xhat
    sums = [jnp.sum(v, 0, keepdims=True) for v in (dnx * (1.0 - ind), dnx * ind, dn * (1.0 - ind), dn * ind)]
    gb_src[0] = jnp.concatenate(sums + [jnp.zeros((4, feats), F32)], axis=0)
    for d in (1, 3, 2):
        send(gb_src.at[0], gb_recv.at[d - 1], gb_send.at[0], gb_sem.at[d - 1], dev("z", d))
    st_src[1, 1] = stat_take(1, 0)
    stat_send(1, "y", 1)
    gb = gb_src[0]
    for d in (1, 3, 2):
        wait(gb_recv.at[d - 1], gb_sem.at[d - 1])
        gb = gb + gb_recv[d - 1]
    gb_src[1] = gb
    send(gb_src.at[1], gb_recv.at[3], gb_send.at[1], gb_sem.at[3], dev("c", 1))
    mean_g, mean_gx = unpack(stat_take(1, 1))
    ig_ref[...] = (
        inv * (dxhat - mean_g / WIDTH - xhat * (mean_gx / WIDTH)) + dy_ref[...].astype(F32)
    ).astype(BF16)
    wait(gb_recv.at[3], gb_sem.at[3])
    gb = gb + gb_recv[3]
    gain_out[...] = gb[0:2]
    bias_out[...] = gb[2:4]
    wait(gb_recv.at[pl.ds(0, 3)], gb_send.at[0])
    wait(gb_recv.at[3], gb_send.at[1])
    wait(dy.at[pl.ds(0, 3 * rows)], z_send.at[0])
    wait(nrm.at[pl.ds(0, 3 * rows)], z_send.at[1])
    wait(dn_recv, z_send.at[2])
    for k, (src, dst) in enumerate(w_pairs):
        wait(dst, w_send.at[k])


def per_device(
    inputs, cotangent, modality, modality_norm_gain, modality_norm_bias, w_gate, w_up, w_down
):
    rows, feats = inputs.shape
    half = feats // 2
    tokens = rows * RING
    hidden = w_gate.shape[1]
    nc = hidden // CHUNK
    sub = rows // RING
    own = lax.dynamic_slice_in_dim(modality, lax.axis_index("ffn") * rows, rows, 0)
    own = jnp.broadcast_to(own.astype(F32)[:, None], (rows, LANES))
    vmem = pl.BlockSpec(memory_space=pltpu.VMEM)
    anyw = pl.BlockSpec(memory_space=pl.ANY)

    def buf(*shape, kind=BF16):
        return pltpu.VMEM(shape, kind)

    def dma(*shape):
        return pltpu.SemaphoreType.DMA(shape)

    scratch = [
        buf(feats, hidden), buf(feats, hidden), buf(2, hidden, half),
        buf(tokens, feats), buf(tokens, feats), buf(feats, tokens),
        buf(tokens, feats, kind=F32), buf(tokens, feats), buf(3, rows, feats),
        buf(nc, 2, 4, 4, sub, LANES), buf(nc, 2, 4, 4, 2 * sub, LANES),
        buf(nc, 2, 4, sub, LANES), buf(nc, 2, 4, 2 * sub, LANES),
        buf(nc, 2, 4, sub, LANES), buf(nc, 2, 4, 2 * sub, LANES),
        buf(nc, 2, 4, sub, LANES), buf(nc, 2, 4, 2 * sub, LANES),
        buf(nc, 2, sub, LANES), buf(nc, 2, 2 * sub, LANES),
        buf(nc, 2, sub, LANES), buf(nc, 2, 2 * sub, LANES),
        buf(nc, 2, sub, LANES), buf(nc, 2, 2 * sub, LANES),
        buf(nc, 2, 4, 4, 3 * sub, LANES),
        buf(2, 3, CHUNK, CHUNK), buf(nc, 3, CHUNK, CHUNK), buf(2, 3, CHUNK, CHUNK, kind=F32),
        buf(2, 3, 8, 256, kind=F32), buf(2, 2, 3, 8, 256, kind=F32),
        buf(2, 8, feats, kind=F32), buf(4, 8, feats, kind=F32),
        dma(3), dma(3), dma(3), dma(3), dma(3, 3), dma(2, 2), dma(2, 2, 3), dma(2), dma(4),
        dma(2, nc, 2), dma(2, nc, 2), dma(2, nc, 2, 4), dma(2, nc, 2, 4),
        dma(nc, 2), dma(nc, 2), dma(nc, 2, 3), dma(nc, 2, 3), dma(2), dma(nc), dma(2, 3),
    ]
    ig, gain_gradient, grad_bias, gg, gu, gd = pl.pallas_call(
        functools.partial(block_kernel, nc),
        out_shape=(
            jax.ShapeDtypeStruct((rows, feats), BF16),
            jax.ShapeDtypeStruct((2, feats), F32),
            jax.ShapeDtypeStruct((2, feats), F32),
            jax.ShapeDtypeStruct((half, hidden), F32),
            jax.ShapeDtypeStruct((half, hidden), F32),
            jax.ShapeDtypeStruct((hidden, half), F32),
        ),
        in_specs=[vmem] * 5 + [anyw] * 3,
        out_specs=(vmem, vmem, vmem, anyw, anyw, anyw),
        scratch_shapes=scratch,
        compiler_params=pltpu.CompilerParams(
            collective_id=0, has_side_effects=True, vmem_limit_bytes=63 * 2**20
        ),
        cost_estimate=pl.CostEstimate(
            flops=16 * tokens * feats * hidden, bytes_accessed=40 * 2**20, transcendentals=tokens * hidden // 16
        ),
        name="ffn_backward",
    )(inputs, cotangent, own, modality_norm_gain, modality_norm_bias, w_gate, w_up, w_down)
    return (ig, gg, gu, gd, gain_gradient, grad_bias)


def solution(mesh):
    return jax.shard_map(
        per_device,
        mesh=mesh,
        in_specs=(
            P(("tok", "ffn"), "hid"),
            P(("tok", "ffn"), "hid"),
            P("tok"),
            P(None, "hid"),
            P(None, "hid"),
            P(("hid", "tok"), "ffn"),
            P(("hid", "tok"), "ffn"),
            P("ffn", ("hid", "tok")),
        ),
        out_specs=(
            P(("tok", "ffn"), "hid"),
            P(("hid", "tok"), "ffn"),
            P(("hid", "tok"), "ffn"),
            P("ffn", ("hid", "tok")),
            P(None, "hid"),
            P(None, "hid"),
        ),
        check_vma=False,
    )
```

```python
import functools

import jax
import jax.numpy as jnp
from jax import lax
from jax.experimental import pallas as pl
from jax.experimental.pallas import tpu as pltpu
from jax.sharding import PartitionSpec as P

WIDTH = 8192
EPS = 1e-05
RING = 4
LANES = 128
CHUNK = 256
AHEAD = 4
SLOTS = 5
MESH = pl.DeviceIdType.MESH
F32 = jnp.float32
BF16 = jnp.bfloat16


def dot_nn(a, b):
    return lax.dot_general(a, b, (((1,), (0,)), ((), ())), preferred_element_type=F32)


def dot_nt(a, b):
    return lax.dot_general(a, b, (((1,), (1,)), ((), ())), preferred_element_type=F32)


def dot_tn(a, b):
    return lax.dot_general(a, b, (((0,), (0,)), ((), ())), preferred_element_type=F32)


def block_kernel(
    n_chunks,
    x_ref, dy_ref, mod_ref, gain_ref, bias_ref, wg_hbm, wu_hbm, wd_hbm,
    ig_ref, gain_out, bias_out, gg_hbm, gu_hbm, gd_hbm,
    wg, wu, wd, dy, nrm, nrm_t, dn_acc, dn_send, dn_recv,
    pd, pg, rld, rlg, fmd, fmg, fpd, fpg, rld2, rlg2, fmd2, fmg2, fpd2, fpg2,
    gat, t_send, t_recv, o_stage, b_stage,
    st_src, st_recv, gb_src, gb_recv,
    w_local, w_send, w_recv, z_send, z_recv, st_send, st_sem, gb_send, gb_sem,
    s1, s2, r1, r2, as1, as2, a1, a2, ts, tr, od,
):
    t = lax.axis_index("tok")
    h = lax.axis_index("hid")
    z = lax.axis_index("ffn")
    y = lax.div(h, RING)
    x = lax.rem(h, RING)
    rows, feats = x_ref.shape
    half = feats // 2
    sub = rows // RING

    def dev(axis, d):
        if axis == "x":
            return (t, y * RING + lax.rem(x + d, RING), z)
        if axis == "y":
            return (t, lax.rem(y + d, RING) * RING + x, z)
        if axis == "z":
            return (t, h, lax.rem(z + d, RING))
        return (1 - t, h, z)

    def send(src, dst, ssem, rsem, to):
        pltpu.make_async_remote_copy(
            src_ref=src, dst_ref=dst, send_sem=ssem, recv_sem=rsem, device_id=to, device_id_type=MESH
        ).start()

    def wait(ref, sem):
        pltpu.make_async_copy(ref, ref, sem).wait()

    barrier = pltpu.get_barrier_semaphore()
    for axis in ("x", "y", "z"):
        for d in (1, 2, 3):
            pl.semaphore_signal(barrier, inc=1, device_id=dev(axis, d), device_id_type=MESH)
    pl.semaphore_signal(barrier, inc=1, device_id=dev("c", 1), device_id_type=MESH)

    mine = pl.ds(pl.multiple_of(t * half, half), half)
    other = pl.ds(pl.multiple_of((1 - t) * half, half), half)
    zrows = pl.ds(pl.multiple_of(z * rows, rows), rows)
    w_pairs = ((wd_hbm, wd.at[t]), (wg_hbm, wg.at[mine]), (wu_hbm, wu.at[mine]))
    for k, (src, dst) in enumerate(w_pairs):
        pltpu.make_async_copy(src, dst, w_local.at[k]).start()
    dy[zrows] = dy_ref[...]
    dn_acc[...] = jnp.zeros_like(dn_acc)

    lane = lax.broadcasted_iota(jnp.int32, (rows, LANES), 1)

    def pack(a, b):
        both = jnp.where(lane == 0, a, jnp.where(lane == 1, b, 0.0))
        both = jnp.concatenate([both, jnp.zeros((256 - rows, LANES), F32)], axis=0)
        return both.T[0:8]

    def unpack(v):
        back = jnp.concatenate([v, jnp.zeros((LANES - 8, 256), F32)], axis=0).T
        return back[0:rows, 0:1], back[0:rows, 1:2]

    def stat_send(use, axis, k):
        for d in (1, 2, 3):
            send(st_src.at[use, k], st_recv.at[use, k, d - 1], st_send.at[use, k], st_sem.at[use, k, d - 1], dev(axis, d))

    def stat_take(use, k):
        total = st_src[use, k]
        for d in (1, 2, 3):
            wait(st_recv.at[use, k, d - 1], st_sem.at[use, k, d - 1])
            total = total + st_recv[use, k, d - 1]
        wait(st_recv.at[use, k], st_send.at[use, k])
        return total

    xv = x_ref[...].astype(F32)
    st_src[0, 0] = pack(jnp.sum(xv, -1, keepdims=True), jnp.sum(xv * xv, -1, keepdims=True))

    pl.semaphore_wait(barrier, 10)

    def zpart(d, first_row, size):
        return pl.ds(pl.multiple_of(lax.rem(z + d, RING) * rows + first_row, 16), size)

    def gather_send(buf, u):
        for d in (1, 3):
            send(buf.at[zrows], buf.at[zrows], z_send.at[u], z_recv.at[u, d - 1], dev("z", d))

    def gather_relay(buf, u):
        for d, start in ((1, 0), (3, rows // 2)):
            wait(buf.at[zrows], z_recv.at[u, d - 1])
            part = buf.at[zpart(RING - d, start, rows // 2)]
            send(part, part, z_send.at[u], z_recv.at[u, 1], dev("z", d))

    def gather_done(buf, u):
        wait(buf.at[zrows], z_recv.at[u, 1])

    gather_send(dy, 0)
    stat_send(0, "x", 0)
    for k, (src, dst) in enumerate(w_pairs):
        send(src, dst, w_send.at[k], w_recv.at[k], dev("c", 1))

    def second_is_one():
        return mod_ref[...] == 1.0

    def gain_selected():
        return jnp.where(second_is_one()[:, 0:1], gain_ref[1:2], gain_ref[0:1])

    def moments(total):
        s, sq = unpack(total)
        mean = s / WIDTH
        return mean, lax.rsqrt(sq / WIDTH - mean * mean + EPS)

    def normalised():
        mean, inv = moments(st_src[0, 2])
        return (x_ref[...].astype(F32) - mean) * inv, inv

    def take_dy():
        gather_done(dy, 0)
        wait(wd.at[t], w_local.at[0])
        wait(wd.at[t], w_recv.at[0])

    def stat_second():
        st_src[0, 1] = stat_take(0, 0)
        stat_send(0, "y", 1)

    def norm_send():
        st_src[0, 2] = stat_take(0, 1)
        xhat, _ = normalised()
        bias = jnp.where(second_is_one()[:, 0:1], bias_ref[1:2], bias_ref[0:1])
        nrm[zrows] = (xhat * gain_selected() + bias).astype(BF16)
        gather_send(nrm, 1)

    def norm_take():
        gather_done(nrm, 1)
        for k in (1, 2):
            wait(wg.at[mine], w_local.at[k])
            wait(wg.at[mine], w_recv.at[k])
        nrm_t[...] = nrm[...].T

    def columns(c):
        return pl.ds(pl.multiple_of(c * CHUNK, CHUNK), CHUNK)

    first = (("x", x, "y", y), ("y", y, "x", x))

    kinds = (
        dict(p=pd, rl=rld, fm=fmd, fp=fpd, rl2=rld2, fm2=fmd2, fp2=fpd2, cut=32, k=0),
        dict(p=pg, rl=rlg, fm=fmg, fp=fpg, rl2=rlg2, fm2=fmg2, fp2=fpg2, cut=48, k=1),
    )

    def ring(p):
        return lax.rem(p + 1, RING), lax.rem(p + 2, RING), lax.rem(p + 3, RING)

    def rs_send(kind, c):
        p, rl, fm, fp, k = kind["p"], kind["rl"], kind["fm"], kind["fp"], kind["k"]
        for o in (0, 1):
            ax, me, _, _ = first[o]
            nxt, opp, prv = ring(me)
            ss = s1.at[k, lax.rem(c, SLOTS), o]
            lo, hi = pl.ds(0, 2), pl.ds(2, 2)
            send(p.at[c, o, opp, lo], rl.at[c, o, lo], ss, r1.at[k, lax.rem(c, SLOTS), o, 0], dev(ax, 1))
            send(p.at[c, o, opp, hi], rl.at[c, o, hi], ss, r1.at[k, lax.rem(c, SLOTS), o, 1], dev(ax, 3))
            send(p.at[c, o, nxt, hi], fm.at[c, o, hi], ss, r1.at[k, lax.rem(c, SLOTS), o, 2], dev(ax, 1))
            send(p.at[c, o, prv, lo], fp.at[c, o, lo], ss, r1.at[k, lax.rem(c, SLOTS), o, 3], dev(ax, 3))

    def rs_relay(kind, c):
        p, rl, fm, fp, k = kind["p"], kind["rl"], kind["fm"], kind["fp"], kind["k"]
        for o in (0, 1):
            ax, me, _, _ = first[o]
            nxt, opp, prv = ring(me)
            ss = s1.at[k, lax.rem(c, SLOTS), o]
            for part, to, d, sem, buf, rsem in (
                (pl.ds(0, 2), nxt, 1, 0, fm, 2),
                (pl.ds(2, 2), prv, 3, 1, fp, 3),
            ):
                wait(rl.at[c, o, part], r1.at[k, lax.rem(c, SLOTS), o, sem])
                p[c, o, to, part] = p[c, o, to, part] + rl[c, o, part]
                send(p.at[c, o, to, part], buf.at[c, o, part], ss, r1.at[k, lax.rem(c, SLOTS), o, rsem], dev(ax, d))

    def rs_turn(kind, c):
        p, fm, fp, k = kind["p"], kind["fm"], kind["fp"], kind["k"]
        rl2, fm2, fp2, cut = kind["rl2"], kind["fm2"], kind["fp2"], kind["cut"]
        size = p.shape[4]
        for o in (0, 1):
            _, me, bx, me2 = first[o]
            wait(fm.at[c, o], r1.at[k, lax.rem(c, SLOTS), o, 2])
            wait(fp.at[c, o], r1.at[k, lax.rem(c, SLOTS), o, 3])
            p[c, o, me] = (p[c, o, me].astype(F32) + fm[c, o].astype(F32) + fp[c, o].astype(F32)).astype(BF16)
            nxt, opp, prv = ring(me2)
            ss = s2.at[k, lax.rem(c, SLOTS), o]
            lo, hi = pl.ds(0, cut), pl.ds(cut, size - cut)
            send(p.at[c, o, me, opp, lo], rl2.at[c, o, lo], ss, r2.at[k, lax.rem(c, SLOTS), o, 0], dev(bx, 1))
            send(p.at[c, o, me, opp, hi], rl2.at[c, o, hi], ss, r2.at[k, lax.rem(c, SLOTS), o, 1], dev(bx, 3))
            send(p.at[c, o, me, nxt, hi], fm2.at[c, o, hi], ss, r2.at[k, lax.rem(c, SLOTS), o, 2], dev(bx, 1))
            send(p.at[c, o, me, prv, lo], fp2.at[c, o, lo], ss, r2.at[k, lax.rem(c, SLOTS), o, 3], dev(bx, 3))

    def rs_relay2(kind, c):
        p, k, cut = kind["p"], kind["k"], kind["cut"]
        rl2, fm2, fp2 = kind["rl2"], kind["fm2"], kind["fp2"]
        size = p.shape[4]
        for o in (0, 1):
            _, me, bx, me2 = first[o]
            nxt, opp, prv = ring(me2)
            ss = s2.at[k, lax.rem(c, SLOTS), o]
            wait(p.at[c, o, pl.ds(0, 3)], s1.at[k, lax.rem(c, SLOTS), o])
            for part, to, d, sem, buf, rsem in (
                (pl.ds(0, cut), nxt, 1, 0, fm2, 2),
                (pl.ds(cut, size - cut), prv, 3, 1, fp2, 3),
            ):
                wait(rl2.at[c, o, part], r2.at[k, lax.rem(c, SLOTS), o, sem])
                p[c, o, me, to, part] = p[c, o, me, to, part] + rl2[c, o, part]
                send(p.at[c, o, me, to, part], buf.at[c, o, part], ss, r2.at[k, lax.rem(c, SLOTS), o, rsem], dev(bx, d))

    def rs_settle(kind, c):
        p, k, fm2, fp2 = kind["p"], kind["k"], kind["fm2"], kind["fp2"]
        for o in (0, 1):
            wait(fm2.at[c, o], r2.at[k, lax.rem(c, SLOTS), o, 2])
            wait(fp2.at[c, o], r2.at[k, lax.rem(c, SLOTS), o, 3])
            wait(p.at[c, o, 0, pl.ds(0, 3)], s2.at[k, lax.rem(c, SLOTS), o])

    def rs_final(kind, c, o):
        p, fm2, fp2 = kind["p"], kind["fm2"], kind["fp2"]
        _, me, _, me2 = first[o]
        return p[c, o, me, me2].astype(F32) + fm2[c, o].astype(F32) + fp2[c, o].astype(F32)

    def d_start(c):
        part = dot_nt(dy[:, 0:half], wd[0, columns(c)]) + dot_nt(dy[:, half:feats], wd[1, columns(c)])
        part = part.astype(BF16)
        for o in (0, 1):
            v = part[:, o * LANES:(o + 1) * LANES]
            for q in range(RING):
                for s in range(RING):
                    r = q * rows + s * sub
                    pd[c, o, q, s] = v[r:r + sub]
        rs_send(kinds[0], c)

    def g_start(c):
        for a, w in ((0, wg), (1, wu)):
            part = dot_nn(nrm[...], w[:, columns(c)]).astype(BF16)
            for o in (0, 1):
                v = part[:, o * LANES:(o + 1) * LANES]
                for q in range(RING):
                    for s in range(RING):
                        r = q * rows + s * sub
                        pg[c, o, q, s, a * sub:(a + 1) * sub] = v[r:r + sub]
        rs_send(kinds[1], c)

    def point(c):
        for o in (0, 1):
            _, me, bx, me2 = first[o]
            dact = rs_final(kinds[0], c, o)
            gu = rs_final(kinds[1], c, o)
            gate, up = gu[0:sub], gu[sub:2 * sub]
            sig = jax.nn.sigmoid(gate)
            silu = gate * sig
            gat[c, o, me, me2, 0:sub] = (silu * up).astype(BF16)
            gat[c, o, me, me2, sub:2 * sub] = (dact * up * sig * (1.0 + gate * (1.0 - sig))).astype(BF16)
            gat[c, o, me, me2, 2 * sub:3 * sub] = (dact * silu).astype(BF16)
            piece = gat.at[c, o, me, me2]
            send(piece, piece, as1.at[lax.rem(c, SLOTS), o], a1.at[lax.rem(c, SLOTS), o, 0], dev(bx, 1))
            send(piece, piece, as1.at[lax.rem(c, SLOTS), o], a1.at[lax.rem(c, SLOTS), o, 1], dev(bx, 3))

    def ag_relay(c):
        for o in (0, 1):
            _, me, bx, me2 = first[o]
            nxt, opp, prv = ring(me2)
            for part, frm, d, sem in ((pl.ds(0, 64), prv, 1, 0), (pl.ds(64, 3 * sub - 64), nxt, 3, 1)):
                wait(gat.at[c, o, me, frm], a1.at[lax.rem(c, SLOTS), o, sem])
                ref = gat.at[c, o, me, frm, part]
                send(ref, ref, as1.at[lax.rem(c, SLOTS), o], a1.at[lax.rem(c, SLOTS), o, 2], dev(bx, d))

    def ag_turn(c):
        for o in (0, 1):
            ax, me, _, me2 = first[o]
            _, opp, _ = ring(me2)
            wait(gat.at[c, o, me, opp], a1.at[lax.rem(c, SLOTS), o, 2])
            ref = gat.at[c, o, me]
            send(ref, ref, as2.at[lax.rem(c, SLOTS), o], a2.at[lax.rem(c, SLOTS), o, 0], dev(ax, 1))
            send(ref, ref, as2.at[lax.rem(c, SLOTS), o], a2.at[lax.rem(c, SLOTS), o, 1], dev(ax, 3))

    def ag_relay2(c):
        for o in (0, 1):
            ax, me, _, _ = first[o]
            nxt, opp, prv = ring(me)
            for part, frm, d, sem in ((pl.ds(0, 2), prv, 1, 0), (pl.ds(2, 2), nxt, 3, 1)):
                wait(gat.at[c, o, frm], a2.at[lax.rem(c, SLOTS), o, sem])
                ref = gat.at[c, o, frm, part]
                send(ref, ref, as2.at[lax.rem(c, SLOTS), o], a2.at[lax.rem(c, SLOTS), o, 2], dev(ax, d))

    def out_copies(c, slot):
        return (
            pltpu.make_async_copy(b_stage.at[slot, 0], gg_hbm.at[:, columns(c)], od.at[slot, 0]),
            pltpu.make_async_copy(b_stage.at[slot, 1], gu_hbm.at[:, columns(c)], od.at[slot, 1]),
            pltpu.make_async_copy(b_stage.at[slot, 2], gd_hbm.at[columns(c)], od.at[slot, 2]),
        )

    def grads(c):
        slot = lax.rem(c, 2)
        for o in (0, 1):
            _, me, _, _ = first[o]
            _, opp, _ = ring(me)
            wait(gat.at[c, o, opp], a2.at[lax.rem(c, SLOTS), o, 2])
            wait(gat.at[c, o, 0, pl.ds(0, 3)], as1.at[lax.rem(c, SLOTS), o])
            wait(gat.at[c, o, pl.ds(0, 3)], as2.at[lax.rem(c, SLOTS), o])

        def whole(a):
            return jnp.concatenate(
                [gat[c, o, :, :, a * sub:(a + 1) * sub].reshape(RING * rows, LANES) for o in (0, 1)], axis=1
            )

        act, dgate, dup = whole(0), whole(1), whole(2)
        dn_acc[...] += dot_nt(dgate, wg[:, columns(c)]) + dot_nt(dup, wu[:, columns(c)])

        @pl.when(c == n_chunks - 1)
        def _():
            dn_send[...] = dn_acc[...].astype(BF16)
            for d in (1, 3, 2):
                rows_to = zpart(d, 0, rows)
                send(dn_send.at[rows_to], dn_recv.at[d - 1], z_send.at[2], z_recv.at[2, d - 1], dev("z", d))

        t_send[slot, 0] = dot_nn(nrm_t[other], dgate).astype(BF16)
        t_send[slot, 1] = dot_nn(nrm_t[other], dup).astype(BF16)
        t_send[slot, 2] = dot_tn(act, dy[:, other]).astype(BF16)
        send(t_send.at[slot], t_recv.at[c], ts.at[slot], tr.at[lax.rem(c, SLOTS)], dev("c", 1))

        o_stage[slot, 0] = dot_nn(nrm_t[mine], dgate)
        o_stage[slot, 1] = dot_nn(nrm_t[mine], dup)
        o_stage[slot, 2] = dot_tn(act, dy[:, mine])

    def finish(c):
        slot = lax.rem(c, 2)
        wait(t_recv.at[c], tr.at[lax.rem(c, SLOTS)])
        wait(t_send.at[slot], ts.at[slot])

        @pl.when(c >= 2)
        def _():
            for copy in out_copies(c, slot):
                copy.wait()

        for k in range(3):
            b_stage[slot, k] = (o_stage[slot, k] + t_recv[c, k].astype(F32)).astype(BF16)
        for copy in out_copies(c, slot):
            copy.start()

    def sweep(count, step):
        lax.fori_loop(0, count, lambda c, _: (step(c), 0)[1], 0)

    d_kind, g_kind = kinds
    stat_second()
    gather_relay(dy, 0)
    norm_send()
    take_dy()
    sweep(AHEAD, d_start)
    gather_relay(nrm, 1)
    sweep(AHEAD - 1, functools.partial(rs_relay, d_kind))
    sweep(AHEAD - 2, functools.partial(rs_turn, d_kind))
    sweep(AHEAD - 3, functools.partial(rs_relay2, d_kind))
    norm_take()

    def tick(i, _):
        def at(off, step):
            c = i - off
            pl.when(jnp.logical_and(c >= 0, c < n_chunks))(lambda: step(c))

        at(9, finish)
        at(8, grads)
        at(7, ag_relay2)
        at(6, ag_turn)
        at(5, ag_relay)
        at(4 - AHEAD, functools.partial(rs_settle, d_kind))
        at(4, functools.partial(rs_settle, g_kind))
        at(4, point)
        at(3, functools.partial(rs_relay2, g_kind))
        at(3 - AHEAD, functools.partial(rs_relay2, d_kind))
        at(2, functools.partial(rs_turn, g_kind))
        at(2 - AHEAD, functools.partial(rs_turn, d_kind))
        at(1, functools.partial(rs_relay, g_kind))
        at(1 - AHEAD, functools.partial(rs_relay, d_kind))
        at(0, g_start)
        at(-AHEAD, d_start)
        return 0

    lax.fori_loop(0, n_chunks + 9, tick, 0)

    for slot in (0, 1):
        for copy in out_copies(0, slot):
            copy.wait()
    xhat, inv = normalised()
    dn = dn_acc[zrows]
    for d in (1, 3, 2):
        wait(dn_recv.at[d - 1], z_recv.at[2, d - 1])
        dn = dn + dn_recv[d - 1].astype(F32)
    dxhat = dn * gain_selected()
    st_src[1, 0] = pack(jnp.sum(dxhat, -1, keepdims=True), jnp.sum(dxhat * xhat, -1, keepdims=True))
    stat_send(1, "x", 0)
    ind = mod_ref[:, 0:1]
    dnx = dn * xhat
    sums = [jnp.sum(v, 0, keepdims=True) for v in (dnx * (1.0 - ind), dnx * ind, dn * (1.0 - ind), dn * ind)]
    gb_src[0] = jnp.concatenate(sums + [jnp.zeros((4, feats), F32)], axis=0)
    for d in (1, 3, 2):
        send(gb_src.at[0], gb_recv.at[d - 1], gb_send.at[0], gb_sem.at[d - 1], dev("z", d))
    st_src[1, 1] = stat_take(1, 0)
    stat_send(1, "y", 1)
    gb = gb_src[0]
    for d in (1, 3, 2):
        wait(gb_recv.at[d - 1], gb_sem.at[d - 1])
        gb = gb + gb_recv[d - 1]
    gb_src[1] = gb
    send(gb_src.at[1], gb_recv.at[3], gb_send.at[1], gb_sem.at[3], dev("c", 1))
    mean_g, mean_gx = unpack(stat_take(1, 1))
    ig_ref[...] = (
        inv * (dxhat - mean_g / WIDTH - xhat * (mean_gx / WIDTH)) + dy_ref[...].astype(F32)
    ).astype(BF16)
    wait(gb_recv.at[3], gb_sem.at[3])
    gb = gb + gb_recv[3]
    gain_out[...] = gb[0:2]
    bias_out[...] = gb[2:4]
    wait(gb_recv.at[pl.ds(0, 3)], gb_send.at[0])
    wait(gb_recv.at[3], gb_send.at[1])
    wait(dy.at[pl.ds(0, 3 * rows)], z_send.at[0])
    wait(nrm.at[pl.ds(0, 3 * rows)], z_send.at[1])
    wait(dn_recv, z_send.at[2])
    for k, (src, dst) in enumerate(w_pairs):
        wait(dst, w_send.at[k])


def write_kernel(*refs):
    for src, dst in zip(refs[:6], refs[6:]):
        dst[...] = src[...].astype(dst.dtype)


def per_device(
    inputs, cotangent, modality, modality_norm_gain, modality_norm_bias, w_gate, w_up, w_down
):
    rows, feats = inputs.shape
    half = feats // 2
    tokens = rows * RING
    hidden = w_gate.shape[1]
    nc = hidden // CHUNK
    sub = rows // RING
    own = lax.dynamic_slice_in_dim(modality, lax.axis_index("ffn") * rows, rows, 0)
    own = jnp.broadcast_to(own.astype(F32)[:, None], (rows, LANES))
    vmem = pl.BlockSpec(memory_space=pltpu.VMEM)
    anyw = pl.BlockSpec(memory_space=pl.ANY)

    def buf(*shape, kind=BF16):
        return pltpu.VMEM(shape, kind)

    def dma(*shape):
        return pltpu.SemaphoreType.DMA(shape)

    scratch = [
        buf(feats, hidden), buf(feats, hidden), buf(2, hidden, half),
        buf(tokens, feats), buf(tokens, feats), buf(feats, tokens),
        buf(tokens, feats, kind=F32), buf(tokens, feats), buf(3, rows, feats),
        buf(nc, 2, 4, 4, sub, LANES), buf(nc, 2, 4, 4, 2 * sub, LANES),
        buf(nc, 2, 4, sub, LANES), buf(nc, 2, 4, 2 * sub, LANES),
        buf(nc, 2, 4, sub, LANES), buf(nc, 2, 4, 2 * sub, LANES),
        buf(nc, 2, 4, sub, LANES), buf(nc, 2, 4, 2 * sub, LANES),
        buf(nc, 2, sub, LANES), buf(nc, 2, 2 * sub, LANES),
        buf(nc, 2, sub, LANES), buf(nc, 2, 2 * sub, LANES),
        buf(nc, 2, sub, LANES), buf(nc, 2, 2 * sub, LANES),
        buf(nc, 2, 4, 4, 3 * sub, LANES),
        buf(2, 3, CHUNK, CHUNK), buf(nc, 3, CHUNK, CHUNK), buf(2, 3, CHUNK, CHUNK, kind=F32), buf(2, 3, CHUNK, CHUNK),
        buf(2, 3, 8, 256, kind=F32), buf(2, 2, 3, 8, 256, kind=F32),
        buf(2, 8, feats, kind=F32), buf(4, 8, feats, kind=F32),
        dma(3), dma(3), dma(3), dma(3), dma(3, 3), dma(2, 2), dma(2, 2, 3), dma(2), dma(4),
        dma(2, SLOTS, 2), dma(2, SLOTS, 2), dma(2, SLOTS, 2, 4), dma(2, SLOTS, 2, 4),
        dma(SLOTS, 2), dma(SLOTS, 2), dma(SLOTS, 2, 3), dma(SLOTS, 2, 3), dma(2), dma(SLOTS), dma(2, 3),
    ]
    results = pl.pallas_call(
        functools.partial(block_kernel, nc),
        out_shape=(
            jax.ShapeDtypeStruct((rows, feats), BF16),
            jax.ShapeDtypeStruct((2, feats), F32),
            jax.ShapeDtypeStruct((2, feats), F32),
            jax.ShapeDtypeStruct((half, hidden), BF16),
            jax.ShapeDtypeStruct((half, hidden), BF16),
            jax.ShapeDtypeStruct((hidden, half), BF16),
        ),
        in_specs=[vmem] * 5 + [anyw] * 3,
        out_specs=(vmem, vmem, vmem, anyw, anyw, anyw),
        scratch_shapes=scratch,
        compiler_params=pltpu.CompilerParams(
            collective_id=0, has_side_effects=True, vmem_limit_bytes=63 * 2**20
        ),
        cost_estimate=pl.CostEstimate(
            flops=16 * tokens * feats * hidden, bytes_accessed=40 * 2**20, transcendentals=tokens * hidden // 16
        ),
        name="ffn_backward",
    )(inputs, cotangent, own, modality_norm_gain, modality_norm_bias, w_gate, w_up, w_down)
    cols = pl.BlockSpec((half, CHUNK), lambda i: (0, i))
    down = pl.BlockSpec((CHUNK, half), lambda i: (i, 0))
    small = [pl.BlockSpec((rows, feats), lambda i: (0, 0))] + [pl.BlockSpec((2, feats), lambda i: (0, 0))] * 2
    ig, gain_gradient, grad_bias, gg, gu, gd = pl.pallas_call(
        write_kernel,
        grid=(nc,),
        out_shape=(
            jax.ShapeDtypeStruct((rows, feats), BF16),
            jax.ShapeDtypeStruct((2, feats), F32),
            jax.ShapeDtypeStruct((2, feats), F32),
            jax.ShapeDtypeStruct((half, hidden), F32),
            jax.ShapeDtypeStruct((half, hidden), F32),
            jax.ShapeDtypeStruct((hidden, half), F32),
        ),
        in_specs=small + [cols, cols, down],
        out_specs=small + [cols, cols, down],
        name="write_results",
    )(*results)
    return (ig, gg, gu, gd, gain_gradient, grad_bias)


def solution(mesh):
    return jax.shard_map(
        per_device,
        mesh=mesh,
        in_specs=(
            P(("tok", "ffn"), "hid"),
            P(("tok", "ffn"), "hid"),
            P("tok"),
            P(None, "hid"),
            P(None, "hid"),
            P(("hid", "tok"), "ffn"),
            P(("hid", "tok"), "ffn"),
            P("ffn", ("hid", "tok")),
        ),
        out_specs=(
            P(("tok", "ffn"), "hid"),
            P(("hid", "tok"), "ffn"),
            P(("hid", "tok"), "ffn"),
            P("ffn", ("hid", "tok")),
            P(None, "hid"),
            P(None, "hid"),
        ),
        check_vma=False,
    )
```

```python
import functools

import jax
import jax.numpy as jnp
from jax import lax
from jax.experimental import pallas as pl
from jax.experimental.pallas import tpu as pltpu
from jax.sharding import PartitionSpec as P

WIDTH = 8192
EPS = 1e-05
RING = 4
LANES = 128
CHUNK = 256
AHEAD = 4
SLOTS = 5
LAG = 5
TAIL = 2
MESH = pl.DeviceIdType.MESH
F32 = jnp.float32
BF16 = jnp.bfloat16


def dot_nn(a, b):
    return lax.dot_general(a, b, (((1,), (0,)), ((), ())), preferred_element_type=F32)


def dot_nt(a, b):
    return lax.dot_general(a, b, (((1,), (1,)), ((), ())), preferred_element_type=F32)


def dot_tn(a, b):
    return lax.dot_general(a, b, (((0,), (0,)), ((), ())), preferred_element_type=F32)


def block_kernel(
    n_chunks,
    x_hbm, dy_hbm, mod_hbm, gain_hbm, bias_hbm, wg_hbm, wu_hbm, wd_hbm,
    ig_ref, gain_out, bias_out, gg_hbm, gu_hbm, gd_hbm,
    x_ref, mod_ref, gain_ref, bias_ref,
    wg, wu, wd, dy, nrm, nrm_t, dn_acc, dn_send, dn_recv,
    pd, pg, rld, rlg, fd, fg, rld2, rlg2, fd2, fg2,
    gat_e, gat_a, t_send, t_recv, o_stage, b_stage,
    st_src, st_recv, st_sum, gb_src, gb_recv, mod_all, mod_col,
    in_sem, w_local, w_send, w_recv, z_send, z_recv, st_send, st_sem, gb_send, gb_sem,
    s1, s2, r1, r2, as1, as2, a1, a2, ts, tr, od,
):
    t = lax.axis_index("tok")
    h = lax.axis_index("hid")
    z = lax.axis_index("ffn")
    y = lax.div(h, RING)
    x = lax.rem(h, RING)
    rows, feats = x_ref.shape
    half = feats // 2
    sub = rows // RING

    def dev(axis, d):
        if axis == "x":
            return (t, y * RING + lax.rem(x + d, RING), z)
        if axis == "y":
            return (t, lax.rem(y + d, RING) * RING + x, z)
        if axis == "h":
            return (t, lax.rem(h + d, RING * RING), z)
        if axis == "z":
            return (t, h, lax.rem(z + d, RING))
        return (1 - t, h, lax.rem(z + d, RING))

    def send(src, dst, ssem, rsem, to):
        pltpu.make_async_remote_copy(
            src_ref=src, dst_ref=dst, send_sem=ssem, recv_sem=rsem, device_id=to, device_id_type=MESH
        ).start()

    def wait(ref, sem):
        pltpu.make_async_copy(ref, ref, sem).wait()

    barrier = pltpu.get_barrier_semaphore()
    peers = [dev("h", d) for d in range(1, 16)] + [dev("z", d) for d in (1, 2, 3)] + [dev("c", d) for d in range(4)]
    for to in peers:
        pl.semaphore_signal(barrier, inc=1, device_id=to, device_id_type=MESH)

    mine = pl.ds(pl.multiple_of(t * half, half), half)
    other = pl.ds(pl.multiple_of((1 - t) * half, half), half)
    zrows = pl.ds(pl.multiple_of(z * rows, rows), rows)
    loads = [
        pltpu.make_async_copy(src, dst, in_sem.at[k])
        for k, (src, dst) in enumerate((
            (dy_hbm, dy.at[zrows]), (x_hbm, x_ref), (mod_hbm, mod_ref), (gain_hbm, gain_ref), (bias_hbm, bias_ref)
        ))
    ]
    for load in loads:
        load.start()
    w_pairs = ((wd_hbm, wd.at[t]), (wg_hbm, wg.at[mine]), (wu_hbm, wu.at[mine]))
    for k, (src, dst) in enumerate(w_pairs):
        pltpu.make_async_copy(src, dst, w_local.at[k]).start()

    lane = lax.broadcasted_iota(jnp.int32, (rows, LANES), 1)

    def pack(a, b):
        both = jnp.where(lane == 0, a, jnp.where(lane == 1, b, 0.0))
        both = jnp.concatenate([both, jnp.zeros((2 * LANES - rows, LANES), F32)], axis=0).T
        return jnp.concatenate([both[0:2, 0:LANES], both[0:2, LANES:], jnp.zeros((4, LANES), F32)], axis=0)

    def unpack(v):
        wide = jnp.concatenate([v[0:2], v[2:4]], axis=1)
        back = jnp.concatenate([wide, jnp.zeros((LANES - 2, 2 * LANES), F32)], axis=0).T
        return back[0:rows, 0:1], back[0:rows, 1:2]

    def stat_send(use):
        for d in range(1, 16):
            send(st_src.at[use], st_recv.at[use, d - 1], st_send.at[use], st_sem.at[use], dev("h", d))

    def stat_take(use):
        wait(st_recv.at[use], st_sem.at[use])
        total = st_src[use]
        for d in range(1, 16):
            total = total + st_recv[use, d - 1]
        wait(st_recv.at[use], st_send.at[use])
        return total

    def zpart(d, first_row, size):
        return pl.ds(pl.multiple_of(lax.rem(z + d, RING) * rows + first_row, 16), size)

    def gather_send(buf, u):
        for d in (1, 3):
            send(buf.at[zrows], buf.at[zrows], z_send.at[u], z_recv.at[u, d - 1], dev("z", d))

    def gather_relay(buf, u):
        for d, start in ((1, 0), (3, rows // 2)):
            wait(buf.at[zrows], z_recv.at[u, d - 1])
            part = buf.at[zpart(RING - d, start, rows // 2)]
            send(part, part, z_send.at[u], z_recv.at[u, 1], dev("z", d))

    def gather_done(buf, u):
        wait(buf.at[zrows], z_recv.at[u, 1])

    loads[0].wait()
    pl.semaphore_wait(barrier, len(peers))
    gather_send(dy, 0)
    loads[1].wait()
    xv = x_ref[...].astype(F32)
    st_src[0] = pack(jnp.sum(xv, -1, keepdims=True), jnp.sum(xv * xv, -1, keepdims=True))
    stat_send(0)
    for k, (src, dst) in enumerate(w_pairs):
        send(src, dst, w_send.at[k], w_recv.at[k], dev("c", 0))
    for load in loads[2:]:
        load.wait()
    mod_all[...] = jnp.broadcast_to(mod_ref[...].astype(F32).reshape(1, RING * rows), (LANES, RING * rows)).T
    mod_col[...] = mod_all[zrows]
    dn_acc[...] = jnp.zeros_like(dn_acc)

    def second_is_one():
        return mod_col[...] == 1.0

    def gain_selected():
        return jnp.where(second_is_one()[:, 0:1], gain_ref[1:2], gain_ref[0:1])

    def moments(total):
        s, sq = unpack(total)
        mean = s / WIDTH
        return mean, lax.rsqrt(sq / WIDTH - mean * mean + EPS)

    def normalised():
        mean, inv = moments(st_sum[...])
        return (x_ref[...].astype(F32) - mean) * inv, inv

    def take_dy():
        gather_done(dy, 0)
        wait(wd.at[t], w_local.at[0])
        wait(wd.at[t], w_recv.at[0])

    def norm_send():
        st_sum[...] = stat_take(0)
        xhat, _ = normalised()
        bias = jnp.where(second_is_one()[:, 0:1], bias_ref[1:2], bias_ref[0:1])
        nrm[zrows] = (xhat * gain_selected() + bias).astype(BF16)
        gather_send(nrm, 1)

    def norm_take():
        gather_done(nrm, 1)
        for k in (1, 2):
            wait(wg.at[mine], w_local.at[k])
            wait(wg.at[mine], w_recv.at[k])

    def turn_normed():
        nrm_t[...] = nrm[...].T

    def columns(c):
        return pl.ds(pl.multiple_of(c * CHUNK, CHUNK), CHUNK)

    first = (("x", x, "y", y), ("y", y, "x", x))

    kinds = (
        dict(p=pd, rl=rld, f=fd, rl2=rld2, f2=fd2, cut=32, k=0),
        dict(p=pg, rl=rlg, f=fg, rl2=rlg2, f2=fg2, cut=48, k=1),
    )

    def ring(p):
        return lax.rem(p + 1, RING), lax.rem(p + 2, RING), lax.rem(p + 3, RING)

    def rs_send(kind, c):
        p, rl, f, k = kind["p"], kind["rl"], kind["f"], kind["k"]
        slot = lax.rem(c, SLOTS)
        lo, hi = pl.ds(0, 2), pl.ds(2, 2)
        ss, relay, last = s1.at[k, slot], r1.at[k, slot, 0], r1.at[k, slot, 1]
        for o in (0, 1):
            ax, me, _, _ = first[o]
            nxt, opp, prv = ring(me)
            send(p.at[c, o, opp, lo], rl.at[c, o, lo], ss, relay, dev(ax, 1))
            send(p.at[c, o, opp, hi], rl.at[c, o, hi], ss, relay, dev(ax, 3))
        for o in (0, 1):
            ax, me, _, _ = first[o]
            nxt, opp, prv = ring(me)
            send(p.at[c, o, nxt, hi], f.at[c, o, 0, hi], ss, last, dev(ax, 1))
            send(p.at[c, o, prv, lo], f.at[c, o, 1, lo], ss, last, dev(ax, 3))

    def rs_relay(kind, c):
        p, rl, f, k = kind["p"], kind["rl"], kind["f"], kind["k"]
        slot = lax.rem(c, SLOTS)
        wait(rl.at[c], r1.at[k, slot, 0])
        for o in (0, 1):
            ax, me, _, _ = first[o]
            nxt, opp, prv = ring(me)
            for part, to, d, side in ((pl.ds(0, 2), nxt, 1, 0), (pl.ds(2, 2), prv, 3, 1)):
                p[c, o, to, part] = p[c, o, to, part] + rl[c, o, part]
                send(p.at[c, o, to, part], f.at[c, o, side, part], s1.at[k, slot], r1.at[k, slot, 1], dev(ax, d))

    def rs_turn(kind, c):
        p, f, rl2, f2, cut, k = kind["p"], kind["f"], kind["rl2"], kind["f2"], kind["cut"], kind["k"]
        slot = lax.rem(c, SLOTS)
        size = p.shape[4]
        lo, hi = pl.ds(0, cut), pl.ds(cut, size - cut)
        ss, relay, last = s2.at[k, slot], r2.at[k, slot, 0], r2.at[k, slot, 1]
        wait(f.at[c], r1.at[k, slot, 1])
        for o in (0, 1):
            _, me, bx, me2 = first[o]
            p[c, o, me] = (p[c, o, me].astype(F32) + f[c, o, 0].astype(F32) + f[c, o, 1].astype(F32)).astype(BF16)
            nxt, opp, prv = ring(me2)
            send(p.at[c, o, me, opp, lo], rl2.at[c, o, lo], ss, relay, dev(bx, 1))
            send(p.at[c, o, me, opp, hi], rl2.at[c, o, hi], ss, relay, dev(bx, 3))
            send(p.at[c, o, me, nxt, hi], f2.at[c, o, 0, hi], ss, last, dev(bx, 1))
            send(p.at[c, o, me, prv, lo], f2.at[c, o, 1, lo], ss, last, dev(bx, 3))

    def rs_relay2(kind, c):
        p, rl2, f2, cut, k = kind["p"], kind["rl2"], kind["f2"], kind["cut"], kind["k"]
        slot = lax.rem(c, SLOTS)
        size = p.shape[4]
        wait(p.at[c, :, pl.ds(0, 3)], s1.at[k, slot])
        wait(rl2.at[c], r2.at[k, slot, 0])
        for o in (0, 1):
            _, me, bx, me2 = first[o]
            nxt, opp, prv = ring(me2)
            for part, to, d, side in ((pl.ds(0, cut), nxt, 1, 0), (pl.ds(cut, size - cut), prv, 3, 1)):
                p[c, o, me, to, part] = p[c, o, me, to, part] + rl2[c, o, part]
                send(p.at[c, o, me, to, part], f2.at[c, o, side, part], s2.at[k, slot], r2.at[k, slot, 1], dev(bx, d))

    def rs_settle(kind, c):
        p, f2, k = kind["p"], kind["f2"], kind["k"]
        slot = lax.rem(c, SLOTS)
        wait(f2.at[c], r2.at[k, slot, 1])
        wait(p.at[c, :, 0, pl.ds(0, 3)], s2.at[k, slot])

    def rs_final(kind, c, o):
        p, f2 = kind["p"], kind["f2"]
        _, me, _, me2 = first[o]
        return p[c, o, me, me2].astype(F32) + f2[c, o, 0].astype(F32) + f2[c, o, 1].astype(F32)

    def d_start(c):
        part = dot_nt(dy[:, 0:half], wd[0, columns(c)]) + dot_nt(dy[:, half:feats], wd[1, columns(c)])
        part = part.astype(BF16)
        for o in (0, 1):
            v = part[:, o * LANES:(o + 1) * LANES]
            for q in range(RING):
                for s in range(RING):
                    r = q * rows + s * sub
                    pd[c, o, q, s] = v[r:r + sub]
        rs_send(kinds[0], c)

    def g_start(c):
        for a, w in ((0, wg), (1, wu)):
            part = dot_nn(nrm[...], w[:, columns(c)]).astype(BF16)
            for o in (0, 1):
                v = part[:, o * LANES:(o + 1) * LANES]
                for q in range(RING):
                    for s in range(RING):
                        r = q * rows + s * sub
                        pg[c, o, q, s, a * sub:(a + 1) * sub] = v[r:r + sub]
        rs_send(kinds[1], c)

    def point(c):
        for o in (0, 1):
            _, me, _, me2 = first[o]
            dact = rs_final(kinds[0], c, o)
            gu = rs_final(kinds[1], c, o)
            gate, up = gu[0:sub], gu[sub:2 * sub]
            sig = jax.nn.sigmoid(gate)
            silu = gate * sig
            gat_a[c, o, me, me2] = (silu * up).astype(BF16)
            gat_e[c, o, me, me2, 0:sub] = (dact * up * sig * (1.0 + gate * (1.0 - sig))).astype(BF16)
            gat_e[c, o, me, me2, sub:2 * sub] = (dact * silu).astype(BF16)

    e_kind = dict(g=gat_e, cut=48, base=0, slots=SLOTS)
    a_kind = dict(g=gat_a, cut=32, base=SLOTS, slots=n_chunks)

    def ag_start(kind, c):
        g, slot = kind["g"], kind["base"] + lax.rem(c, kind["slots"])
        for o in (0, 1):
            _, me, bx, me2 = first[o]
            piece = g.at[c, o, me, me2]
            for d in (1, 3):
                send(piece, piece, as1.at[slot], a1.at[slot, 0], dev(bx, d))

    def ag_relay(kind, c):
        g, slot, cut = kind["g"], kind["base"] + lax.rem(c, kind["slots"]), kind["cut"]
        size = g.shape[4]
        wait(g.at[c, :, 0, pl.ds(0, 2)], a1.at[slot, 0])
        for o in (0, 1):
            _, me, bx, me2 = first[o]
            nxt, opp, prv = ring(me2)
            for part, frm, d in ((pl.ds(0, cut), prv, 1), (pl.ds(cut, size - cut), nxt, 3)):
                ref = g.at[c, o, me, frm, part]
                send(ref, ref, as1.at[slot], a1.at[slot, 1], dev(bx, d))

    def ag_turn(kind, c):
        g, slot = kind["g"], kind["base"] + lax.rem(c, kind["slots"])
        wait(g.at[c, :, 0, 0], a1.at[slot, 1])
        for o in (0, 1):
            ax, me, _, _ = first[o]
            ref = g.at[c, o, me]
            for d in (1, 3):
                send(ref, ref, as2.at[slot], a2.at[slot, 0], dev(ax, d))

    def ag_relay2(kind, c):
        g, slot = kind["g"], kind["base"] + lax.rem(c, kind["slots"])
        wait(g.at[c, :, pl.ds(0, 2)], a2.at[slot, 0])
        for o in (0, 1):
            ax, me, _, _ = first[o]
            nxt, opp, prv = ring(me)
            for part, frm, d in ((pl.ds(0, 2), prv, 1), (pl.ds(2, 2), nxt, 3)):
                ref = g.at[c, o, frm, part]
                send(ref, ref, as2.at[slot], a2.at[slot, 1], dev(ax, d))

    def ag_whole(kind, c, a):
        g = kind["g"]
        return jnp.concatenate(
            [g[c, o, :, :, a * sub:(a + 1) * sub].reshape(RING * rows, LANES) for o in (0, 1)], axis=1
        )

    def ag_done(kind, c):
        g, slot = kind["g"], kind["base"] + lax.rem(c, kind["slots"])
        wait(g.at[c, :, 0], a2.at[slot, 1])
        wait(g.at[c, :, 0, pl.ds(0, 3)], as1.at[slot])
        wait(g.at[c, :, pl.ds(0, 3)], as2.at[slot])

    def out_copies(which, c, slot):
        if which == 0:
            return (
                pltpu.make_async_copy(b_stage.at[slot, 0], gg_hbm.at[:, columns(c)], od.at[slot, 0]),
                pltpu.make_async_copy(b_stage.at[slot, 1], gu_hbm.at[:, columns(c)], od.at[slot, 1]),
            )
        return (pltpu.make_async_copy(b_stage.at[slot, 2], gd_hbm.at[columns(c)], od.at[slot, 2]),)

    lanes_of = (pl.ds(0, 2), pl.ds(2, 1))

    def swap(which, c):
        slot, part = lax.rem(c, 2), lanes_of[which]
        send(t_send.at[slot, part], t_recv.at[c, part], ts.at[which, slot], tr.at[which, lax.rem(c, SLOTS)], dev("c", 0))

    def grads_e(c):
        slot = lax.rem(c, 2)
        ag_done(e_kind, c)
        dgate, dup = ag_whole(e_kind, c, 0), ag_whole(e_kind, c, 1)
        dn_acc[...] += dot_nt(dgate, wg[:, columns(c)]) + dot_nt(dup, wu[:, columns(c)])

        @pl.when(c == n_chunks - 1)
        def _():
            dn_send[...] = dn_acc[...].astype(BF16)
            for d in (1, 3, 2):
                rows_to = zpart(d, 0, rows)
                send(dn_send.at[rows_to], dn_recv.at[d - 1], z_send.at[2], z_recv.at[2, d - 1], dev("z", d))

        t_send[slot, 0] = dot_nn(nrm_t[other], dgate).astype(BF16)
        t_send[slot, 1] = dot_nn(nrm_t[other], dup).astype(BF16)
        swap(0, c)
        o_stage[slot, 0] = dot_nn(nrm_t[mine], dgate)
        o_stage[slot, 1] = dot_nn(nrm_t[mine], dup)

    def grads_a(c):
        slot = lax.rem(c, 2)
        ag_done(a_kind, c)
        act = ag_whole(a_kind, c, 0)
        t_send[slot, 2] = dot_tn(act, dy[:, other]).astype(BF16)
        swap(1, c)
        o_stage[slot, 2] = dot_tn(act, dy[:, mine])

    def grads_a_finish(c):
        grads_a(c)
        pl.when(c > 0)(lambda: finish(1, c - 1))

    def finish(which, c):
        slot, part = lax.rem(c, 2), lanes_of[which]
        wait(t_recv.at[c, part], tr.at[which, lax.rem(c, SLOTS)])
        wait(t_send.at[slot, part], ts.at[which, slot])

        @pl.when(c >= 2)
        def _():
            for copy in out_copies(which, c, slot):
                copy.wait()

        for k in ((0, 1), (2,))[which]:
            b_stage[slot, k] = (o_stage[slot, k] + t_recv[c, k].astype(F32)).astype(BF16)
        for copy in out_copies(which, c, slot):
            copy.start()

    def sweep(count, step):
        lax.fori_loop(0, count, lambda c, _: (step(c), 0)[1], 0)

    d_kind, g_kind = kinds
    gather_relay(dy, 0)
    norm_send()
    take_dy()
    sweep(AHEAD, d_start)
    gather_relay(nrm, 1)
    sweep(AHEAD - 1, functools.partial(rs_relay, d_kind))
    sweep(AHEAD - 2, functools.partial(rs_turn, d_kind))
    sweep(AHEAD - 3, functools.partial(rs_relay2, d_kind))
    norm_take()

    def tail_sum():
        dn = dn_acc[zrows]
        for d in (1, 3, 2):
            wait(dn_recv.at[d - 1], z_recv.at[2, d - 1])
            dn = dn + dn_recv[d - 1].astype(F32)
        xhat, _ = normalised()
        dxhat = dn * gain_selected()
        ind = mod_col[:, 0:1]
        dnx = dn * xhat
        sums = [jnp.sum(v, 0, keepdims=True) for v in (dnx * (1.0 - ind), dnx * ind, dn * (1.0 - ind), dn * ind)]
        st_src[1] = pack(jnp.sum(dxhat, -1, keepdims=True), jnp.sum(dxhat * xhat, -1, keepdims=True))
        gb_src[...] = jnp.concatenate(sums + [jnp.zeros((4, feats), F32)], axis=0)
        stat_send(1)
        for d in (1, 2, 3):
            send(gb_src, gb_recv.at[d - 1], gb_send, gb_sem, dev("z", d))
        for d in range(4):
            send(gb_src, gb_recv.at[3 + d], gb_send, gb_sem, dev("c", d))
        dn_acc[zrows] = dxhat

    def tail_last():
        mean_g, mean_gx = unpack(stat_take(1))
        xhat, inv = normalised()
        ig_ref[...] = (
            inv * (dn_acc[zrows] - mean_g / WIDTH - xhat * (mean_gx / WIDTH)) + dy[zrows].astype(F32)
        ).astype(BF16)
        wait(gb_recv, gb_sem)
        gb = gb_src[...]
        for d in range(7):
            gb = gb + gb_recv[d]
        gain_out[...] = gb[0:2]
        bias_out[...] = gb[2:4]
        wait(gb_recv, gb_send)

    def tick(i, _):
        def at(off, step, *kind):
            c = i - off
            pl.when(jnp.logical_and(c >= 0, c < n_chunks))(lambda: step(*kind, c))

        def late(off, step, *kind):
            c = i - off - LAG
            count = jnp.where(i - off == n_chunks, LAG, jnp.where(i - off > n_chunks, 0, jnp.where(c >= 0, 1, 0)))
            lax.fori_loop(c, c + count, lambda k, _: (step(*kind, k), 0)[1], 0)

        at(0, g_start)
        at(-AHEAD, d_start)
        pl.when(i == 1)(turn_normed)
        at(1, rs_relay, g_kind)
        at(1 - AHEAD, rs_relay, d_kind)
        at(2, rs_turn, g_kind)
        at(2 - AHEAD, rs_turn, d_kind)
        at(3, rs_relay2, g_kind)
        at(3 - AHEAD, rs_relay2, d_kind)
        at(4, rs_settle, g_kind)
        at(4 - AHEAD, rs_settle, d_kind)
        at(4, point)
        at(4, ag_start, e_kind)
        late(4, ag_start, a_kind)
        at(5, ag_relay, e_kind)
        late(5, ag_relay, a_kind)
        at(6, ag_turn, e_kind)
        late(6, ag_turn, a_kind)
        at(7, ag_relay2, e_kind)
        late(7, ag_relay2, a_kind)
        at(8, grads_e)
        late(8, grads_a_finish)
        at(9, finish, 0)
        pl.when(i == n_chunks + 7 + TAIL)(tail_sum)
        pl.when(i == n_chunks + 8 + TAIL)(tail_last)
        return 0

    lax.fori_loop(0, n_chunks + 9 + TAIL, tick, 0)
    finish(1, n_chunks - 1)

    for slot in (0, 1):
        for which in (0, 1):
            for copy in out_copies(which, 0, slot):
                copy.wait()
    wait(dy.at[pl.ds(0, 3 * rows)], z_send.at[0])
    wait(nrm.at[pl.ds(0, 3 * rows)], z_send.at[1])
    wait(dn_recv, z_send.at[2])
    for k, (src, dst) in enumerate(w_pairs):
        wait(dst, w_send.at[k])


def write_kernel(*refs):
    for src, dst in zip(refs[:6], refs[6:]):
        dst[...] = src[...].astype(dst.dtype)


def per_device(
    inputs, cotangent, modality, modality_norm_gain, modality_norm_bias, w_gate, w_up, w_down
):
    rows, feats = inputs.shape
    half = feats // 2
    tokens = rows * RING
    hidden = w_gate.shape[1]
    nc = hidden // CHUNK
    sub = rows // RING
    vmem = pl.BlockSpec(memory_space=pltpu.VMEM)
    anyw = pl.BlockSpec(memory_space=pl.ANY)

    def buf(*shape, kind=BF16):
        return pltpu.VMEM(shape, kind)

    def dma(*shape):
        return pltpu.SemaphoreType.DMA(shape)

    one = pltpu.SemaphoreType.DMA

    scratch = [
        buf(rows, feats), buf(tokens, kind=jnp.int32), buf(2, feats, kind=F32), buf(2, feats, kind=F32),
        buf(feats, hidden), buf(feats, hidden), buf(2, hidden, half),
        buf(tokens, feats), buf(tokens, feats), buf(feats, tokens),
        buf(tokens, feats, kind=F32), buf(tokens, feats), buf(3, rows, feats),
        buf(nc, 2, 4, 4, sub, LANES), buf(nc, 2, 4, 4, 2 * sub, LANES),
        buf(nc, 2, 4, sub, LANES), buf(nc, 2, 4, 2 * sub, LANES),
        buf(nc, 2, 2, 4, sub, LANES), buf(nc, 2, 2, 4, 2 * sub, LANES),
        buf(nc, 2, sub, LANES), buf(nc, 2, 2 * sub, LANES),
        buf(nc, 2, 2, sub, LANES), buf(nc, 2, 2, 2 * sub, LANES),
        buf(nc, 2, 4, 4, 2 * sub, LANES), buf(nc, 2, 4, 4, sub, LANES),
        buf(2, 3, CHUNK, CHUNK), buf(nc, 3, CHUNK, CHUNK), buf(2, 3, CHUNK, CHUNK, kind=F32), buf(2, 3, CHUNK, CHUNK),
        buf(2, 8, LANES, kind=F32), buf(2, 15, 8, LANES, kind=F32), buf(8, LANES, kind=F32),
        buf(8, feats, kind=F32), buf(7, 8, feats, kind=F32),
        buf(tokens, LANES, kind=F32), buf(rows, LANES, kind=F32),
        dma(5), dma(3), dma(3), dma(3), dma(3), dma(3, 3), dma(2), dma(2), one, one,
        dma(2, SLOTS), dma(2, SLOTS), dma(2, SLOTS, 2), dma(2, SLOTS, 2),
        dma(SLOTS + nc), dma(SLOTS + nc), dma(SLOTS + nc, 2), dma(SLOTS + nc, 2),
        dma(2, 2), dma(2, SLOTS), dma(2, 3),
    ]
    results = pl.pallas_call(
        functools.partial(block_kernel, nc),
        out_shape=(
            jax.ShapeDtypeStruct((rows, feats), BF16),
            jax.ShapeDtypeStruct((2, feats), F32),
            jax.ShapeDtypeStruct((2, feats), F32),
            jax.ShapeDtypeStruct((half, hidden), BF16),
            jax.ShapeDtypeStruct((half, hidden), BF16),
            jax.ShapeDtypeStruct((hidden, half), BF16),
        ),
        in_specs=[anyw] * 8,
        out_specs=(vmem, vmem, vmem, anyw, anyw, anyw),
        scratch_shapes=scratch,
        compiler_params=pltpu.CompilerParams(
            collective_id=0, has_side_effects=True, vmem_limit_bytes=63 * 2**20
        ),
        cost_estimate=pl.CostEstimate(
            flops=16 * tokens * feats * hidden, bytes_accessed=40 * 2**20, transcendentals=tokens * hidden // 16
        ),
        name="ffn_backward",
    )(inputs, cotangent, modality, modality_norm_gain, modality_norm_bias, w_gate, w_up, w_down)
    cols = pl.BlockSpec((half // 4, hidden), lambda i: (i, 0))
    down = pl.BlockSpec((hidden // 4, half), lambda i: (i, 0))
    small = [pl.BlockSpec((rows, feats), lambda i: (0, 0))] + [pl.BlockSpec((2, feats), lambda i: (0, 0))] * 2
    ig, gain_gradient, grad_bias, gg, gu, gd = pl.pallas_call(
        write_kernel,
        grid=(4,),
        out_shape=(
            jax.ShapeDtypeStruct((rows, feats), BF16),
            jax.ShapeDtypeStruct((2, feats), F32),
            jax.ShapeDtypeStruct((2, feats), F32),
            jax.ShapeDtypeStruct((half, hidden), F32),
            jax.ShapeDtypeStruct((half, hidden), F32),
            jax.ShapeDtypeStruct((hidden, half), F32),
        ),
        in_specs=small + [cols, cols, down],
        out_specs=small + [cols, cols, down],
        compiler_params=pltpu.CompilerParams(vmem_limit_bytes=63 * 2**20),
        name="write_results",
    )(*results)
    return (ig, gg, gu, gd, gain_gradient, grad_bias)


def solution(mesh):
    return jax.shard_map(
        per_device,
        mesh=mesh,
        in_specs=(
            P(("tok", "ffn"), "hid"),
            P(("tok", "ffn"), "hid"),
            P("tok"),
            P(None, "hid"),
            P(None, "hid"),
            P(("hid", "tok"), "ffn"),
            P(("hid", "tok"), "ffn"),
            P("ffn", ("hid", "tok")),
        ),
        out_specs=(
            P(("tok", "ffn"), "hid"),
            P(("hid", "tok"), "ffn"),
            P(("hid", "tok"), "ffn"),
            P("ffn", ("hid", "tok")),
            P(None, "hid"),
            P(None, "hid"),
        ),
        check_vma=False,
    )
```

```python
import functools

import jax
import jax.numpy as jnp
from jax import lax
from jax.experimental import pallas as pl
from jax.experimental.pallas import tpu as pltpu
from jax.sharding import PartitionSpec as P

WIDTH = 8192
EPS = 1e-05
RING = 4
LANES = 128
CHUNK = 256
AHEAD = 4
SLOTS = 5
LAG = 5
AFTER = 3
MESH = pl.DeviceIdType.MESH
F32 = jnp.float32
BF16 = jnp.bfloat16


def dot_nn(a, b):
    return lax.dot_general(a, b, (((1,), (0,)), ((), ())), preferred_element_type=F32)


def dot_nt(a, b):
    return lax.dot_general(a, b, (((1,), (1,)), ((), ())), preferred_element_type=F32)


def block_kernel(
    n_chunks,
    x_hbm, dy_hbm, mod_hbm, gain_hbm, bias_hbm, wg_hbm, wu_hbm, wd_hbm,
    ig_ref, gain_out, bias_out, gg_hbm, gu_hbm, gd_hbm,
    x_ref, mod_ref, gain_ref, bias_ref,
    wg, wu, wd, dy, dy_t, nrm, nrm_t, dn_acc, dn_send, dn_recv,
    pd, pg, rld, rlg, fd, fg, rld2, rlg2, fd2, fg2,
    gat_e, gat_a, t_send, t_recv, o_stage, b_stage,
    st_src, st_recv, st_sum, gb_src, gb_recv, mod_all, mod_col,
    in_sem, w_local, w_send, w_recv, z_send, z_recv, st_send, st_sem, gb_send, gb_sem,
    s1, s2, r1, r2, as1, as2, a1, a2, ts, tr, od,
):
    t = lax.axis_index("tok")
    h = lax.axis_index("hid")
    z = lax.axis_index("ffn")
    y = lax.div(h, RING)
    x = lax.rem(h, RING)
    rows, feats = x_ref.shape
    half = feats // 2
    sub = rows // RING

    def dev(axis, d):
        if axis == "x":
            return (t, y * RING + lax.rem(x + d, RING), z)
        if axis == "y":
            return (t, lax.rem(y + d, RING) * RING + x, z)
        if axis == "h":
            return (t, lax.rem(h + d, RING * RING), z)
        if axis == "z":
            return (t, h, lax.rem(z + d, RING))
        return (1 - t, h, lax.rem(z + d, RING))

    def send(src, dst, ssem, rsem, to):
        pltpu.make_async_remote_copy(
            src_ref=src, dst_ref=dst, send_sem=ssem, recv_sem=rsem, device_id=to, device_id_type=MESH
        ).start()

    def wait(ref, sem):
        pltpu.make_async_copy(ref, ref, sem).wait()

    barrier = pltpu.get_barrier_semaphore()
    peers = [dev("h", d) for d in range(1, 16)] + [dev("z", d) for d in (1, 2, 3)] + [dev("c", d) for d in range(4)]
    for to in peers:
        pl.semaphore_signal(barrier, inc=1, device_id=to, device_id_type=MESH)

    mine = pl.ds(pl.multiple_of(t * half, half), half)
    other = pl.ds(pl.multiple_of((1 - t) * half, half), half)
    zrows = pl.ds(pl.multiple_of(z * rows, rows), rows)
    loads = [
        pltpu.make_async_copy(src, dst, in_sem.at[k])
        for k, (src, dst) in enumerate((
            (dy_hbm, dy.at[zrows]), (x_hbm, x_ref), (mod_hbm, mod_ref), (gain_hbm, gain_ref), (bias_hbm, bias_ref)
        ))
    ]
    for load in loads:
        load.start()
    w_pairs = ((wd_hbm, wd.at[t]), (wg_hbm, wg.at[mine]), (wu_hbm, wu.at[mine]))
    for k, (src, dst) in enumerate(w_pairs):
        pltpu.make_async_copy(src, dst, w_local.at[k]).start()

    lane = lax.broadcasted_iota(jnp.int32, (rows, LANES), 1)

    def pack(a, b):
        both = jnp.where(lane == 0, a, jnp.where(lane == 1, b, 0.0))
        both = jnp.concatenate([both, jnp.zeros((2 * LANES - rows, LANES), F32)], axis=0).T
        return jnp.concatenate([both[0:2, 0:LANES], both[0:2, LANES:], jnp.zeros((4, LANES), F32)], axis=0)

    def unpack(v):
        wide = jnp.concatenate([v[0:2], v[2:4]], axis=1)
        back = jnp.concatenate([wide, jnp.zeros((LANES - 2, 2 * LANES), F32)], axis=0).T
        return back[0:rows, 0:1], back[0:rows, 1:2]

    def stat_send(use):
        for d in range(1, 16):
            send(st_src.at[use], st_recv.at[use, d - 1], st_send.at[use], st_sem.at[use], dev("h", d))

    def stat_take(use):
        wait(st_recv.at[use], st_sem.at[use])
        total = st_src[use]
        for d in range(1, 16):
            total = total + st_recv[use, d - 1]
        wait(st_recv.at[use], st_send.at[use])
        return total

    def zpart(d, first_row, size):
        return pl.ds(pl.multiple_of(lax.rem(z + d, RING) * rows + first_row, 16), size)

    def gather_send(buf, u):
        for d in (1, 3):
            send(buf.at[zrows], buf.at[zrows], z_send.at[u], z_recv.at[u, d - 1], dev("z", d))

    def gather_relay(buf, u):
        for d, start in ((1, 0), (3, rows // 2)):
            wait(buf.at[zrows], z_recv.at[u, d - 1])
            part = buf.at[zpart(RING - d, start, rows // 2)]
            send(part, part, z_send.at[u], z_recv.at[u, 1], dev("z", d))

    def gather_done(buf, u):
        wait(buf.at[zrows], z_recv.at[u, 1])

    loads[0].wait()
    pl.semaphore_wait(barrier, len(peers))
    gather_send(dy, 0)
    loads[1].wait()
    xv = x_ref[...].astype(F32)
    st_src[0] = pack(jnp.sum(xv, -1, keepdims=True), jnp.sum(xv * xv, -1, keepdims=True))
    stat_send(0)
    for k, (src, dst) in enumerate(w_pairs):
        send(src, dst, w_send.at[k], w_recv.at[k], dev("c", 0))
    for load in loads[2:]:
        load.wait()
    mod_all[...] = jnp.broadcast_to(mod_ref[...].astype(F32).reshape(1, RING * rows), (LANES, RING * rows)).T
    mod_col[...] = mod_all[zrows]
    dn_acc[...] = jnp.zeros_like(dn_acc)

    def second_is_one():
        return mod_col[...] == 1.0

    def gain_selected():
        return jnp.where(second_is_one()[:, 0:1], gain_ref[1:2], gain_ref[0:1])

    def moments(total):
        s, sq = unpack(total)
        mean = s / WIDTH
        return mean, lax.rsqrt(sq / WIDTH - mean * mean + EPS)

    def normalised():
        mean, inv = moments(st_sum[...])
        return (x_ref[...].astype(F32) - mean) * inv, inv

    def take_dy():
        gather_done(dy, 0)
        wait(wd.at[t], w_local.at[0])
        wait(wd.at[t], w_recv.at[0])

    def norm_send():
        st_sum[...] = stat_take(0)
        xhat, _ = normalised()
        bias = jnp.where(second_is_one()[:, 0:1], bias_ref[1:2], bias_ref[0:1])
        nrm[zrows] = (xhat * gain_selected() + bias).astype(BF16)
        gather_send(nrm, 1)

    def norm_take():
        gather_done(nrm, 1)
        for k in (1, 2):
            wait(wg.at[mine], w_local.at[k])
            wait(wg.at[mine], w_recv.at[k])

    def turn_normed():
        nrm_t[...] = nrm[...].T

    def turn_dy():
        dy_t[...] = dy[...].T

    def columns(c):
        return pl.ds(pl.multiple_of(c * CHUNK, CHUNK), CHUNK)

    first = (("x", x, "y", y), ("y", y, "x", x))

    kinds = (
        dict(p=pd, rl=rld, f=fd, rl2=rld2, f2=fd2, cut=32, k=0),
        dict(p=pg, rl=rlg, f=fg, rl2=rlg2, f2=fg2, cut=48, k=1),
    )

    def ring(p):
        return lax.rem(p + 1, RING), lax.rem(p + 2, RING), lax.rem(p + 3, RING)

    def rs_send(kind, c):
        p, rl, f, k = kind["p"], kind["rl"], kind["f"], kind["k"]
        slot = lax.rem(c, SLOTS)
        lo, hi = pl.ds(0, 2), pl.ds(2, 2)
        ss, relay, last = s1.at[k, slot], r1.at[k, slot, 0], r1.at[k, slot, 1]
        for o in (0, 1):
            ax, me, _, _ = first[o]
            nxt, opp, prv = ring(me)
            send(p.at[c, o, opp, lo], rl.at[c, o, lo], ss, relay, dev(ax, 1))
            send(p.at[c, o, opp, hi], rl.at[c, o, hi], ss, relay, dev(ax, 3))
        for o in (0, 1):
            ax, me, _, _ = first[o]
            nxt, opp, prv = ring(me)
            send(p.at[c, o, nxt, hi], f.at[c, o, 0, hi], ss, last, dev(ax, 1))
            send(p.at[c, o, prv, lo], f.at[c, o, 1, lo], ss, last, dev(ax, 3))

    def rs_relay(kind, c):
        p, rl, f, k = kind["p"], kind["rl"], kind["f"], kind["k"]
        slot = lax.rem(c, SLOTS)
        wait(rl.at[c], r1.at[k, slot, 0])
        for o in (0, 1):
            ax, me, _, _ = first[o]
            nxt, opp, prv = ring(me)
            for part, to, d, side in ((pl.ds(0, 2), nxt, 1, 0), (pl.ds(2, 2), prv, 3, 1)):
                p[c, o, to, part] = p[c, o, to, part] + rl[c, o, part]
                send(p.at[c, o, to, part], f.at[c, o, side, part], s1.at[k, slot], r1.at[k, slot, 1], dev(ax, d))

    def rs_turn(kind, c):
        p, f, rl2, f2, cut, k = kind["p"], kind["f"], kind["rl2"], kind["f2"], kind["cut"], kind["k"]
        slot = lax.rem(c, SLOTS)
        size = p.shape[4]
        lo, hi = pl.ds(0, cut), pl.ds(cut, size - cut)
        ss, relay, last = s2.at[k, slot], r2.at[k, slot, 0], r2.at[k, slot, 1]
        wait(f.at[c], r1.at[k, slot, 1])
        for o in (0, 1):
            _, me, bx, me2 = first[o]
            p[c, o, me] = (p[c, o, me].astype(F32) + f[c, o, 0].astype(F32) + f[c, o, 1].astype(F32)).astype(BF16)
            nxt, opp, prv = ring(me2)
            send(p.at[c, o, me, opp, lo], rl2.at[c, o, lo], ss, relay, dev(bx, 1))
            send(p.at[c, o, me, opp, hi], rl2.at[c, o, hi], ss, relay, dev(bx, 3))
            send(p.at[c, o, me, nxt, hi], f2.at[c, o, 0, hi], ss, last, dev(bx, 1))
            send(p.at[c, o, me, prv, lo], f2.at[c, o, 1, lo], ss, last, dev(bx, 3))

    def rs_relay2(kind, c):
        p, rl2, f2, cut, k = kind["p"], kind["rl2"], kind["f2"], kind["cut"], kind["k"]
        slot = lax.rem(c, SLOTS)
        size = p.shape[4]
        wait(p.at[c, :, pl.ds(0, 3)], s1.at[k, slot])
        wait(rl2.at[c], r2.at[k, slot, 0])
        for o in (0, 1):
            _, me, bx, me2 = first[o]
            nxt, opp, prv = ring(me2)
            for part, to, d, side in ((pl.ds(0, cut), nxt, 1, 0), (pl.ds(cut, size - cut), prv, 3, 1)):
                p[c, o, me, to, part] = p[c, o, me, to, part] + rl2[c, o, part]
                send(p.at[c, o, me, to, part], f2.at[c, o, side, part], s2.at[k, slot], r2.at[k, slot, 1], dev(bx, d))

    def rs_settle(kind, c):
        p, f2, k = kind["p"], kind["f2"], kind["k"]
        slot = lax.rem(c, SLOTS)
        wait(f2.at[c], r2.at[k, slot, 1])
        wait(p.at[c, :, 0, pl.ds(0, 3)], s2.at[k, slot])

    def rs_final(kind, c, o):
        p, f2 = kind["p"], kind["f2"]
        _, me, _, me2 = first[o]
        return p[c, o, me, me2].astype(F32) + f2[c, o, 0].astype(F32) + f2[c, o, 1].astype(F32)

    def d_start(c):
        part = dot_nt(dy[:, 0:half], wd[0, columns(c)]) + dot_nt(dy[:, half:feats], wd[1, columns(c)])
        part = part.astype(BF16)
        for o in (0, 1):
            v = part[:, o * LANES:(o + 1) * LANES]
            for q in range(RING):
                for s in range(RING):
                    r = q * rows + s * sub
                    pd[c, o, q, s] = v[r:r + sub]
        rs_send(kinds[0], c)

    def g_start(c):
        for a, w in ((0, wg), (1, wu)):
            part = dot_nn(nrm[...], w[:, columns(c)]).astype(BF16)
            for o in (0, 1):
                v = part[:, o * LANES:(o + 1) * LANES]
                for q in range(RING):
                    for s in range(RING):
                        r = q * rows + s * sub
                        pg[c, o, q, s, a * sub:(a + 1) * sub] = v[r:r + sub]
        rs_send(kinds[1], c)

    def point(c):
        for o in (0, 1):
            _, me, _, me2 = first[o]
            dact = rs_final(kinds[0], c, o)
            gu = rs_final(kinds[1], c, o)
            gate, up = gu[0:sub], gu[sub:2 * sub]
            sig = jax.nn.sigmoid(gate)
            silu = gate * sig
            gat_a[c, o, me, me2] = (silu * up).astype(BF16)
            gat_e[c, o, me, me2, 0:sub] = (dact * up * sig * (1.0 + gate * (1.0 - sig))).astype(BF16)
            gat_e[c, o, me, me2, sub:2 * sub] = (dact * silu).astype(BF16)

    e_kind = dict(g=gat_e, cut=48, base=0, slots=SLOTS)
    a_kind = dict(g=gat_a, cut=32, base=SLOTS, slots=n_chunks)

    def ag_start(kind, c):
        g, slot = kind["g"], kind["base"] + lax.rem(c, kind["slots"])
        for o in (0, 1):
            _, me, bx, me2 = first[o]
            piece = g.at[c, o, me, me2]
            for d in (1, 3):
                send(piece, piece, as1.at[slot], a1.at[slot, 0], dev(bx, d))

    def ag_relay(kind, c):
        g, slot, cut = kind["g"], kind["base"] + lax.rem(c, kind["slots"]), kind["cut"]
        size = g.shape[4]
        wait(g.at[c, :, 0, pl.ds(0, 2)], a1.at[slot, 0])
        for o in (0, 1):
            _, me, bx, me2 = first[o]
            nxt, opp, prv = ring(me2)
            for part, frm, d in ((pl.ds(0, cut), prv, 1), (pl.ds(cut, size - cut), nxt, 3)):
                ref = g.at[c, o, me, frm, part]
                send(ref, ref, as1.at[slot], a1.at[slot, 1], dev(bx, d))

    def ag_turn(kind, c):
        g, slot = kind["g"], kind["base"] + lax.rem(c, kind["slots"])
        wait(g.at[c, :, 0, 0], a1.at[slot, 1])
        for o in (0, 1):
            ax, me, _, _ = first[o]
            ref = g.at[c, o, me]
            for d in (1, 3):
                send(ref, ref, as2.at[slot], a2.at[slot, 0], dev(ax, d))

    def ag_relay2(kind, c):
        g, slot = kind["g"], kind["base"] + lax.rem(c, kind["slots"])
        wait(g.at[c, :, pl.ds(0, 2)], a2.at[slot, 0])
        for o in (0, 1):
            ax, me, _, _ = first[o]
            nxt, opp, prv = ring(me)
            for part, frm, d in ((pl.ds(0, 2), prv, 1), (pl.ds(2, 2), nxt, 3)):
                ref = g.at[c, o, frm, part]
                send(ref, ref, as2.at[slot], a2.at[slot, 1], dev(ax, d))

    def ag_whole(kind, c, a):
        g = kind["g"]
        return jnp.concatenate(
            [g[c, o, :, :, a * sub:(a + 1) * sub].reshape(RING * rows, LANES) for o in (0, 1)], axis=1
        )

    def ag_done(kind, c):
        g, slot = kind["g"], kind["base"] + lax.rem(c, kind["slots"])
        wait(g.at[c, :, 0], a2.at[slot, 1])
        wait(g.at[c, :, 0, pl.ds(0, 3)], as1.at[slot])
        wait(g.at[c, :, pl.ds(0, 3)], as2.at[slot])

    def out_copies(which, c, slot):
        if which == 0:
            return (
                pltpu.make_async_copy(b_stage.at[slot, 0], gg_hbm.at[:, columns(c)], od.at[slot, 0]),
                pltpu.make_async_copy(b_stage.at[slot, 1], gu_hbm.at[:, columns(c)], od.at[slot, 1]),
            )
        return (pltpu.make_async_copy(b_stage.at[slot, 2], gd_hbm.at[columns(c)], od.at[slot, 2]),)

    lanes_of = (pl.ds(0, 2), pl.ds(2, 1))

    def swap(which, c):
        slot, part = lax.rem(c, 2), lanes_of[which]
        send(t_send.at[slot, part], t_recv.at[c, part], ts.at[which, slot], tr.at[which, lax.rem(c, SLOTS)], dev("c", 0))

    def grads_e(c):
        slot = lax.rem(c, 2)
        ag_done(e_kind, c)
        dgate, dup = ag_whole(e_kind, c, 0), ag_whole(e_kind, c, 1)
        dn_acc[...] += dot_nt(dgate, wg[:, columns(c)]) + dot_nt(dup, wu[:, columns(c)])

        @pl.when(c == n_chunks - 1)
        def _():
            dn_send[...] = dn_acc[...].astype(BF16)
            for d in (1, 3, 2):
                rows_to = zpart(d, 0, rows)
                send(dn_send.at[rows_to], dn_recv.at[d - 1], z_send.at[2], z_recv.at[2, d - 1], dev("z", d))

        t_send[slot, 0] = dot_nn(nrm_t[other], dgate).astype(BF16)
        t_send[slot, 1] = dot_nn(nrm_t[other], dup).astype(BF16)
        swap(0, c)
        o_stage[slot, 0] = dot_nn(nrm_t[mine], dgate)
        o_stage[slot, 1] = dot_nn(nrm_t[mine], dup)

    def grads_a(c):
        slot = lax.rem(c, 2)
        ag_done(a_kind, c)
        act = ag_whole(a_kind, c, 0)
        t_send[slot, 2] = dot_nn(dy_t[other], act).astype(BF16)
        swap(1, c)
        o_stage[slot, 2] = dot_nn(dy_t[mine], act)

    def grads_a_finish(c):
        grads_a(c)
        pl.when(c > 0)(lambda: finish(1, c - 1))

    def finish(which, c):
        slot, part = lax.rem(c, 2), lanes_of[which]
        wait(t_recv.at[c, part], tr.at[which, lax.rem(c, SLOTS)])
        wait(t_send.at[slot, part], ts.at[which, slot])

        @pl.when(c >= 2)
        def _():
            for copy in out_copies(which, c, slot):
                copy.wait()

        for k in ((0, 1), (2,))[which]:
            total = (o_stage[slot, k] + t_recv[c, k].astype(F32)).astype(BF16)
            b_stage[slot, k] = total.T if k == 2 else total
        for copy in out_copies(which, c, slot):
            copy.start()

    def sweep(count, step):
        lax.fori_loop(0, count, lambda c, _: (step(c), 0)[1], 0)

    d_kind, g_kind = kinds
    gather_relay(dy, 0)
    norm_send()
    take_dy()
    sweep(AHEAD, d_start)
    gather_relay(nrm, 1)
    sweep(AHEAD - 1, functools.partial(rs_relay, d_kind))
    sweep(AHEAD - 2, functools.partial(rs_turn, d_kind))
    sweep(AHEAD - 3, functools.partial(rs_relay2, d_kind))
    norm_take()

    def tail_sum():
        dn = dn_acc[zrows]
        for d in (1, 3, 2):
            wait(dn_recv.at[d - 1], z_recv.at[2, d - 1])
            dn = dn + dn_recv[d - 1].astype(F32)
        xhat, _ = normalised()
        dxhat = dn * gain_selected()
        ind = mod_col[:, 0:1]
        dnx = dn * xhat
        sums = [jnp.sum(v, 0, keepdims=True) for v in (dnx * (1.0 - ind), dnx * ind, dn * (1.0 - ind), dn * ind)]
        st_src[1] = pack(jnp.sum(dxhat, -1, keepdims=True), jnp.sum(dxhat * xhat, -1, keepdims=True))
        gb_src[...] = jnp.concatenate(sums + [jnp.zeros((4, feats), F32)], axis=0)
        stat_send(1)
        for d in (1, 2, 3):
            send(gb_src, gb_recv.at[d - 1], gb_send, gb_sem, dev("z", d))
        for d in range(4):
            send(gb_src, gb_recv.at[3 + d], gb_send, gb_sem, dev("c", d))
        dn_acc[zrows] = dxhat

    def tail_last():
        mean_g, mean_gx = unpack(stat_take(1))
        xhat, inv = normalised()
        ig_ref[...] = (
            inv * (dn_acc[zrows] - mean_g / WIDTH - xhat * (mean_gx / WIDTH)) + dy[zrows].astype(F32)
        ).astype(BF16)
        wait(gb_recv, gb_sem)
        gb = gb_src[...]
        for d in range(7):
            gb = gb + gb_recv[d]
        gain_out[...] = gb[0:2]
        bias_out[...] = gb[2:4]
        wait(gb_recv, gb_send)

    def tick(i, _):
        def at(off, step, *kind):
            c = i - off
            pl.when(jnp.logical_and(c >= 0, c < n_chunks))(lambda: step(*kind, c))

        def late(off, step, *kind):
            c = i - off - LAG
            count = jnp.where(i - off == n_chunks, LAG, jnp.where(i - off > n_chunks, 0, jnp.where(c >= 0, 1, 0)))
            lax.fori_loop(c, c + count, lambda k, _: (step(*kind, k), 0)[1], 0)

        at(0, g_start)
        at(-AHEAD, d_start)
        pl.when(i == 2)(turn_normed)
        pl.when(i == 4)(turn_dy)
        at(1, rs_relay, g_kind)
        at(1 - AHEAD, rs_relay, d_kind)
        at(2, rs_turn, g_kind)
        at(2 - AHEAD, rs_turn, d_kind)
        at(3, rs_relay2, g_kind)
        at(3 - AHEAD, rs_relay2, d_kind)
        at(4, rs_settle, g_kind)
        at(4 - AHEAD, rs_settle, d_kind)
        at(4, point)
        at(4, ag_start, e_kind)
        at(4, ag_start, a_kind)
        at(5, ag_relay, e_kind)
        at(5, ag_relay, a_kind)
        at(6, ag_turn, e_kind)
        at(7, ag_relay2, e_kind)
        at(8, grads_e)
        at(9, finish, 0)
        late(6, ag_turn, a_kind)
        late(7, ag_relay2, a_kind)
        late(8, grads_a_finish)
        return 0

    lax.fori_loop(0, n_chunks + 8, tick, 0)

    def rest(first_chunk, last_chunk):
        lax.fori_loop(first_chunk, last_chunk, lambda c, _: (grads_a_finish(c), 0)[1], 0)

    finish(0, n_chunks - 1)
    rest(n_chunks - LAG, n_chunks - AFTER)
    tail_sum()
    rest(n_chunks - AFTER, n_chunks)
    finish(1, n_chunks - 1)
    tail_last()

    for slot in (0, 1):
        for which in (0, 1):
            for copy in out_copies(which, 0, slot):
                copy.wait()
    wait(dy.at[pl.ds(0, 3 * rows)], z_send.at[0])
    wait(nrm.at[pl.ds(0, 3 * rows)], z_send.at[1])
    wait(dn_recv, z_send.at[2])
    for k, (src, dst) in enumerate(w_pairs):
        wait(dst, w_send.at[k])


def write_kernel(*refs):
    for src, dst in zip(refs[:6], refs[6:]):
        dst[...] = src[...].astype(dst.dtype)


def per_device(
    inputs, cotangent, modality, modality_norm_gain, modality_norm_bias, w_gate, w_up, w_down
):
    rows, feats = inputs.shape
    half = feats // 2
    tokens = rows * RING
    hidden = w_gate.shape[1]
    nc = hidden // CHUNK
    sub = rows // RING
    vmem = pl.BlockSpec(memory_space=pltpu.VMEM)
    anyw = pl.BlockSpec(memory_space=pl.ANY)

    def buf(*shape, kind=BF16):
        return pltpu.VMEM(shape, kind)

    def dma(*shape):
        return pltpu.SemaphoreType.DMA(shape)

    one = pltpu.SemaphoreType.DMA

    scratch = [
        buf(rows, feats), buf(tokens, kind=jnp.int32), buf(2, feats, kind=F32), buf(2, feats, kind=F32),
        buf(feats, hidden), buf(feats, hidden), buf(2, hidden, half),
        buf(tokens, feats), buf(feats, tokens), buf(tokens, feats), buf(feats, tokens),
        buf(tokens, feats, kind=F32), buf(tokens, feats), buf(3, rows, feats),
        buf(nc, 2, 4, 4, sub, LANES), buf(nc, 2, 4, 4, 2 * sub, LANES),
        buf(nc, 2, 4, sub, LANES), buf(nc, 2, 4, 2 * sub, LANES),
        buf(nc, 2, 2, 4, sub, LANES), buf(nc, 2, 2, 4, 2 * sub, LANES),
        buf(nc, 2, sub, LANES), buf(nc, 2, 2 * sub, LANES),
        buf(nc, 2, 2, sub, LANES), buf(nc, 2, 2, 2 * sub, LANES),
        buf(nc, 2, 4, 4, 2 * sub, LANES), buf(nc, 2, 4, 4, sub, LANES),
        buf(2, 3, CHUNK, CHUNK), buf(nc, 3, CHUNK, CHUNK), buf(2, 3, CHUNK, CHUNK, kind=F32), buf(2, 3, CHUNK, CHUNK),
        buf(2, 8, LANES, kind=F32), buf(2, 15, 8, LANES, kind=F32), buf(8, LANES, kind=F32),
        buf(8, feats, kind=F32), buf(7, 8, feats, kind=F32),
        buf(tokens, LANES, kind=F32), buf(rows, LANES, kind=F32),
        dma(5), dma(3), dma(3), dma(3), dma(3), dma(3, 3), dma(2), dma(2), one, one,
        dma(2, SLOTS), dma(2, SLOTS), dma(2, SLOTS, 2), dma(2, SLOTS, 2),
        dma(SLOTS + nc), dma(SLOTS + nc), dma(SLOTS + nc, 2), dma(SLOTS + nc, 2),
        dma(2, 2), dma(2, SLOTS), dma(2, 3),
    ]
    results = pl.pallas_call(
        functools.partial(block_kernel, nc),
        out_shape=(
            jax.ShapeDtypeStruct((rows, feats), BF16),
            jax.ShapeDtypeStruct((2, feats), F32),
            jax.ShapeDtypeStruct((2, feats), F32),
            jax.ShapeDtypeStruct((half, hidden), BF16),
            jax.ShapeDtypeStruct((half, hidden), BF16),
            jax.ShapeDtypeStruct((hidden, half), BF16),
        ),
        in_specs=[anyw] * 8,
        out_specs=(vmem, vmem, vmem, anyw, anyw, anyw),
        scratch_shapes=scratch,
        compiler_params=pltpu.CompilerParams(
            collective_id=0, has_side_effects=True, vmem_limit_bytes=63 * 2**20
        ),
        cost_estimate=pl.CostEstimate(
            flops=16 * tokens * feats * hidden, bytes_accessed=40 * 2**20, transcendentals=tokens * hidden // 16
        ),
        name="ffn_backward",
    )(inputs, cotangent, modality, modality_norm_gain, modality_norm_bias, w_gate, w_up, w_down)
    cols = pl.BlockSpec((half // 4, hidden), lambda i: (i, 0))
    down = pl.BlockSpec((hidden // 4, half), lambda i: (i, 0))
    small = [pl.BlockSpec((rows, feats), lambda i: (0, 0))] + [pl.BlockSpec((2, feats), lambda i: (0, 0))] * 2
    ig, gain_gradient, grad_bias, gg, gu, gd = pl.pallas_call(
        write_kernel,
        grid=(4,),
        out_shape=(
            jax.ShapeDtypeStruct((rows, feats), BF16),
            jax.ShapeDtypeStruct((2, feats), F32),
            jax.ShapeDtypeStruct((2, feats), F32),
            jax.ShapeDtypeStruct((half, hidden), F32),
            jax.ShapeDtypeStruct((half, hidden), F32),
            jax.ShapeDtypeStruct((hidden, half), F32),
        ),
        in_specs=small + [cols, cols, down],
        out_specs=small + [cols, cols, down],
        compiler_params=pltpu.CompilerParams(vmem_limit_bytes=63 * 2**20),
        name="write_results",
    )(*results)
    return (ig, gg, gu, gd, gain_gradient, grad_bias)


def solution(mesh):
    return jax.shard_map(
        per_device,
        mesh=mesh,
        in_specs=(
            P(("tok", "ffn"), "hid"),
            P(("tok", "ffn"), "hid"),
            P("tok"),
            P(None, "hid"),
            P(None, "hid"),
            P(("hid", "tok"), "ffn"),
            P(("hid", "tok"), "ffn"),
            P("ffn", ("hid", "tok")),
        ),
        out_specs=(
            P(("tok", "ffn"), "hid"),
            P(("hid", "tok"), "ffn"),
            P(("hid", "tok"), "ffn"),
            P("ffn", ("hid", "tok")),
            P(None, "hid"),
            P(None, "hid"),
        ),
        check_vma=False,
    )
```

```python
import functools

import jax
import jax.numpy as jnp
from jax import lax
from jax.experimental import pallas as pl
from jax.experimental.pallas import tpu as pltpu
from jax.sharding import PartitionSpec as P

WIDTH = 8192
EPS = 1e-05
RING = 4
LANES = 128
CHUNK = 256
AHEAD = 4
SLOTS = 5
LAG = 5
AFTER = 3
MESH = pl.DeviceIdType.MESH
F32 = jnp.float32
BF16 = jnp.bfloat16


def dot_nn(a, b):
    return lax.dot_general(a, b, (((1,), (0,)), ((), ())), preferred_element_type=F32)


def dot_nt(a, b):
    return lax.dot_general(a, b, (((1,), (1,)), ((), ())), preferred_element_type=F32)


def block_kernel(
    n_chunks,
    x_hbm, dy_hbm, mod_hbm, gain_hbm, bias_hbm, wg_hbm, wu_hbm, wd_hbm,
    ig_ref, gain_out, bias_out, gg_hbm, gu_hbm, gd_hbm,
    x_ref, mod_ref, gain_ref, bias_ref,
    wg, wu, wd, dy, dy_t, nrm, nrm_t, dn_acc, dn_send, dn_recv,
    pd, pg, rld, rlg, fd, fg, rld2, rlg2, fd2, fg2,
    gat_e, gat_a, t_send, t_recv, o_stage, b_stage,
    st_src, st_recv, st_sum, gb_src, gb_recv, mod_all, mod_col,
    in_sem, w_local, w_send, w_recv, z_send, z_recv, st_send, st_sem, gb_send, gb_sem,
    s1, s2, r1, r2, as1, as2, a1, a2, ts, tr, od,
):
    t = lax.axis_index("tok")
    h = lax.axis_index("hid")
    z = lax.axis_index("ffn")
    y = lax.div(h, RING)
    x = lax.rem(h, RING)
    rows, feats = x_ref.shape
    half = feats // 2
    sub = rows // RING

    def dev(axis, d):
        if axis == "x":
            return (t, y * RING + lax.rem(x + d, RING), z)
        if axis == "y":
            return (t, lax.rem(y + d, RING) * RING + x, z)
        if axis == "h":
            return (t, lax.rem(h + d, RING * RING), z)
        if axis == "z":
            return (t, h, lax.rem(z + d, RING))
        return (1 - t, h, lax.rem(z + d, RING))

    def send(src, dst, ssem, rsem, to):
        pltpu.make_async_remote_copy(
            src_ref=src, dst_ref=dst, send_sem=ssem, recv_sem=rsem, device_id=to, device_id_type=MESH
        ).start()

    def wait(ref, sem):
        pltpu.make_async_copy(ref, ref, sem).wait()

    barrier = pltpu.get_barrier_semaphore()
    peers = [dev("h", d) for d in range(1, 16)] + [dev("z", d) for d in (1, 2, 3)] + [dev("c", d) for d in range(4)]
    for to in peers:
        pl.semaphore_signal(barrier, inc=1, device_id=to, device_id_type=MESH)

    mine = pl.ds(pl.multiple_of(t * half, half), half)
    other = pl.ds(pl.multiple_of((1 - t) * half, half), half)
    zrows = pl.ds(pl.multiple_of(z * rows, rows), rows)
    loads = [
        pltpu.make_async_copy(src, dst, in_sem.at[k])
        for k, (src, dst) in enumerate((
            (dy_hbm, dy.at[zrows]), (x_hbm, x_ref), (mod_hbm, mod_ref), (gain_hbm, gain_ref), (bias_hbm, bias_ref)
        ))
    ]
    for load in loads:
        load.start()
    w_pairs = ((wd_hbm, wd.at[t]), (wg_hbm, wg.at[mine]), (wu_hbm, wu.at[mine]))
    for k, (src, dst) in enumerate(w_pairs):
        pltpu.make_async_copy(src, dst, w_local.at[k]).start()

    lane = lax.broadcasted_iota(jnp.int32, (rows, LANES), 1)

    def pack(a, b):
        both = jnp.where(lane == 0, a, jnp.where(lane == 1, b, 0.0))
        both = jnp.concatenate([both, jnp.zeros((2 * LANES - rows, LANES), F32)], axis=0).T
        return jnp.concatenate([both[0:2, 0:LANES], both[0:2, LANES:], jnp.zeros((4, LANES), F32)], axis=0)

    def unpack(v):
        wide = jnp.concatenate([v[0:2], v[2:4]], axis=1)
        back = jnp.concatenate([wide, jnp.zeros((LANES - 2, 2 * LANES), F32)], axis=0).T
        return back[0:rows, 0:1], back[0:rows, 1:2]

    def stat_send(use):
        for d in range(1, 16):
            send(st_src.at[use], st_recv.at[use, d - 1], st_send.at[use], st_sem.at[use], dev("h", d))

    def stat_take(use):
        wait(st_recv.at[use], st_sem.at[use])
        total = st_src[use]
        for d in range(1, 16):
            total = total + st_recv[use, d - 1]
        wait(st_recv.at[use], st_send.at[use])
        return total

    def zpart(d, first_row, size):
        return pl.ds(pl.multiple_of(lax.rem(z + d, RING) * rows + first_row, 16), size)

    def gather_send(buf, u):
        for d in (1, 3):
            send(buf.at[zrows], buf.at[zrows], z_send.at[u], z_recv.at[u, d - 1], dev("z", d))

    def gather_relay(buf, u):
        for d, start in ((1, 0), (3, rows // 2)):
            wait(buf.at[zrows], z_recv.at[u, d - 1])
            part = buf.at[zpart(RING - d, start, rows // 2)]
            send(part, part, z_send.at[u], z_recv.at[u, 1], dev("z", d))

    def gather_done(buf, u):
        wait(buf.at[zrows], z_recv.at[u, 1])

    loads[0].wait()
    pl.semaphore_wait(barrier, len(peers))
    gather_send(dy, 0)
    loads[1].wait()
    xv = x_ref[...].astype(F32)
    st_src[0] = pack(jnp.sum(xv, -1, keepdims=True), jnp.sum(xv * xv, -1, keepdims=True))
    stat_send(0)
    for k, (src, dst) in enumerate(w_pairs):
        send(src, dst, w_send.at[k], w_recv.at[k], dev("c", 0))
    for load in loads[2:]:
        load.wait()
    mod_all[...] = jnp.broadcast_to(mod_ref[...].astype(F32).reshape(1, RING * rows), (LANES, RING * rows)).T
    mod_col[...] = mod_all[zrows]
    dn_acc[...] = jnp.zeros_like(dn_acc)

    def second_is_one():
        return mod_col[...] == 1.0

    def gain_selected():
        return jnp.where(second_is_one()[:, 0:1], gain_ref[1:2], gain_ref[0:1])

    def moments(total):
        s, sq = unpack(total)
        mean = s / WIDTH
        return mean, lax.rsqrt(sq / WIDTH - mean * mean + EPS)

    def normalised():
        mean, inv = moments(st_sum[...])
        return (x_ref[...].astype(F32) - mean) * inv, inv

    def take_dy():
        gather_done(dy, 0)
        wait(wd.at[t], w_local.at[0])
        wait(wd.at[t], w_recv.at[0])

    def norm_send():
        st_sum[...] = stat_take(0)
        xhat, _ = normalised()
        bias = jnp.where(second_is_one()[:, 0:1], bias_ref[1:2], bias_ref[0:1])
        nrm[zrows] = (xhat * gain_selected() + bias).astype(BF16)
        gather_send(nrm, 1)

    def norm_take():
        gather_done(nrm, 1)
        for k in (1, 2):
            wait(wg.at[mine], w_local.at[k])
            wait(wg.at[mine], w_recv.at[k])

    def turn_normed():
        nrm_t[...] = nrm[...].T

    def turn_dy():
        dy_t[...] = dy[...].T

    def columns(c):
        return pl.ds(pl.multiple_of(c * CHUNK, CHUNK), CHUNK)

    first = (("x", x, "y", y), ("y", y, "x", x))

    kinds = (
        dict(p=pd, rl=rld, f=fd, rl2=rld2, f2=fd2, cut=32, k=0),
        dict(p=pg, rl=rlg, f=fg, rl2=rlg2, f2=fg2, cut=48, k=1),
    )

    def ring(p):
        return lax.rem(p + 1, RING), lax.rem(p + 2, RING), lax.rem(p + 3, RING)

    def rs_send(kind, c):
        p, rl, f, k = kind["p"], kind["rl"], kind["f"], kind["k"]
        slot = lax.rem(c, SLOTS)
        lo, hi = pl.ds(0, 2), pl.ds(2, 2)
        ss, relay, last = s1.at[k, slot], r1.at[k, slot, 0], r1.at[k, slot, 1]
        for o in (0, 1):
            ax, me, _, _ = first[o]
            nxt, opp, prv = ring(me)
            send(p.at[c, o, opp, lo], rl.at[c, o, lo], ss, relay, dev(ax, 1))
            send(p.at[c, o, opp, hi], rl.at[c, o, hi], ss, relay, dev(ax, 3))
        for o in (0, 1):
            ax, me, _, _ = first[o]
            nxt, opp, prv = ring(me)
            send(p.at[c, o, nxt, hi], f.at[c, o, 0, hi], ss, last, dev(ax, 1))
            send(p.at[c, o, prv, lo], f.at[c, o, 1, lo], ss, last, dev(ax, 3))

    def rs_relay(kind, c):
        p, rl, f, k = kind["p"], kind["rl"], kind["f"], kind["k"]
        slot = lax.rem(c, SLOTS)
        wait(rl.at[c], r1.at[k, slot, 0])
        for o in (0, 1):
            ax, me, _, _ = first[o]
            nxt, opp, prv = ring(me)
            for part, to, d, side in ((pl.ds(0, 2), nxt, 1, 0), (pl.ds(2, 2), prv, 3, 1)):
                p[c, o, to, part] = p[c, o, to, part] + rl[c, o, part]
                send(p.at[c, o, to, part], f.at[c, o, side, part], s1.at[k, slot], r1.at[k, slot, 1], dev(ax, d))

    def rs_turn(kind, c):
        p, f, rl2, f2, cut, k = kind["p"], kind["f"], kind["rl2"], kind["f2"], kind["cut"], kind["k"]
        slot = lax.rem(c, SLOTS)
        size = p.shape[4]
        lo, hi = pl.ds(0, cut), pl.ds(cut, size - cut)
        ss, relay, last = s2.at[k, slot], r2.at[k, slot, 0], r2.at[k, slot, 1]
        wait(f.at[c], r1.at[k, slot, 1])
        for o in (0, 1):
            _, me, bx, me2 = first[o]
            p[c, o, me] = (p[c, o, me].astype(F32) + f[c, o, 0].astype(F32) + f[c, o, 1].astype(F32)).astype(BF16)
            nxt, opp, prv = ring(me2)
            send(p.at[c, o, me, opp, lo], rl2.at[c, o, lo], ss, relay, dev(bx, 1))
            send(p.at[c, o, me, opp, hi], rl2.at[c, o, hi], ss, relay, dev(bx, 3))
            send(p.at[c, o, me, nxt, hi], f2.at[c, o, 0, hi], ss, last, dev(bx, 1))
            send(p.at[c, o, me, prv, lo], f2.at[c, o, 1, lo], ss, last, dev(bx, 3))

    def rs_relay2(kind, c):
        p, rl2, f2, cut, k = kind["p"], kind["rl2"], kind["f2"], kind["cut"], kind["k"]
        slot = lax.rem(c, SLOTS)
        size = p.shape[4]
        wait(p.at[c, :, pl.ds(0, 3)], s1.at[k, slot])
        wait(rl2.at[c], r2.at[k, slot, 0])
        for o in (0, 1):
            _, me, bx, me2 = first[o]
            nxt, opp, prv = ring(me2)
            for part, to, d, side in ((pl.ds(0, cut), nxt, 1, 0), (pl.ds(cut, size - cut), prv, 3, 1)):
                p[c, o, me, to, part] = p[c, o, me, to, part] + rl2[c, o, part]
                send(p.at[c, o, me, to, part], f2.at[c, o, side, part], s2.at[k, slot], r2.at[k, slot, 1], dev(bx, d))

    def rs_settle(kind, c):
        p, f2, k = kind["p"], kind["f2"], kind["k"]
        slot = lax.rem(c, SLOTS)
        wait(f2.at[c], r2.at[k, slot, 1])
        wait(p.at[c, :, 0, pl.ds(0, 3)], s2.at[k, slot])

    def rs_final(kind, c, o):
        p, f2 = kind["p"], kind["f2"]
        _, me, _, me2 = first[o]
        return p[c, o, me, me2].astype(F32) + f2[c, o, 0].astype(F32) + f2[c, o, 1].astype(F32)

    def d_start(c):
        part = dot_nt(dy[:, 0:half], wd[0, columns(c)]) + dot_nt(dy[:, half:feats], wd[1, columns(c)])
        part = part.astype(BF16)
        for o in (0, 1):
            v = part[:, o * LANES:(o + 1) * LANES]
            for q in range(RING):
                for s in range(RING):
                    r = q * rows + s * sub
                    pd[c, o, q, s] = v[r:r + sub]
        rs_send(kinds[0], c)

    def g_start(c):
        for a, w in ((0, wg), (1, wu)):
            part = dot_nn(nrm[...], w[:, columns(c)]).astype(BF16)
            for o in (0, 1):
                v = part[:, o * LANES:(o + 1) * LANES]
                for q in range(RING):
                    for s in range(RING):
                        r = q * rows + s * sub
                        pg[c, o, q, s, a * sub:(a + 1) * sub] = v[r:r + sub]
        rs_send(kinds[1], c)

    def point(c):
        for o in (0, 1):
            _, me, _, me2 = first[o]
            dact = rs_final(kinds[0], c, o)
            gu = rs_final(kinds[1], c, o)
            gate, up = gu[0:sub], gu[sub:2 * sub]
            sig = jax.nn.sigmoid(gate)
            silu = gate * sig
            gat_a[c, o, me, me2] = (silu * up).astype(BF16)
            gat_e[c, o, me, me2, 0:sub] = (dact * up * sig * (1.0 + gate * (1.0 - sig))).astype(BF16)
            gat_e[c, o, me, me2, sub:2 * sub] = (dact * silu).astype(BF16)

    e_kind = dict(g=gat_e, cut=48, base=0, slots=SLOTS)
    a_kind = dict(g=gat_a, cut=32, base=SLOTS, slots=n_chunks)

    def ag_start(kind, c):
        g, slot = kind["g"], kind["base"] + lax.rem(c, kind["slots"])
        for o in (0, 1):
            _, me, bx, me2 = first[o]
            piece = g.at[c, o, me, me2]
            for d in (1, 3):
                send(piece, piece, as1.at[slot], a1.at[slot, 0], dev(bx, d))

    def ag_relay(kind, c):
        g, slot, cut = kind["g"], kind["base"] + lax.rem(c, kind["slots"]), kind["cut"]
        size = g.shape[4]
        wait(g.at[c, :, 0, pl.ds(0, 2)], a1.at[slot, 0])
        for o in (0, 1):
            _, me, bx, me2 = first[o]
            nxt, opp, prv = ring(me2)
            for part, frm, d in ((pl.ds(0, cut), prv, 1), (pl.ds(cut, size - cut), nxt, 3)):
                ref = g.at[c, o, me, frm, part]
                send(ref, ref, as1.at[slot], a1.at[slot, 1], dev(bx, d))

    def ag_turn(kind, c):
        g, slot = kind["g"], kind["base"] + lax.rem(c, kind["slots"])
        wait(g.at[c, :, 0, 0], a1.at[slot, 1])
        for o in (0, 1):
            ax, me, _, _ = first[o]
            ref = g.at[c, o, me]
            for d in (1, 3):
                send(ref, ref, as2.at[slot], a2.at[slot, 0], dev(ax, d))

    def ag_relay2(kind, c):
        g, slot = kind["g"], kind["base"] + lax.rem(c, kind["slots"])
        wait(g.at[c, :, pl.ds(0, 2)], a2.at[slot, 0])
        for o in (0, 1):
            ax, me, _, _ = first[o]
            nxt, opp, prv = ring(me)
            for part, frm, d in ((pl.ds(0, 2), prv, 1), (pl.ds(2, 2), nxt, 3)):
                ref = g.at[c, o, frm, part]
                send(ref, ref, as2.at[slot], a2.at[slot, 1], dev(ax, d))

    def ag_whole(kind, c, a):
        g = kind["g"]
        return jnp.concatenate(
            [g[c, o, :, :, a * sub:(a + 1) * sub].reshape(RING * rows, LANES) for o in (0, 1)], axis=1
        )

    def ag_done(kind, c):
        g, slot = kind["g"], kind["base"] + lax.rem(c, kind["slots"])
        wait(g.at[c, :, 0], a2.at[slot, 1])
        wait(g.at[c, :, 0, pl.ds(0, 3)], as1.at[slot])
        wait(g.at[c, :, pl.ds(0, 3)], as2.at[slot])

    def out_copies(which, c, slot):
        if which == 0:
            return (
                pltpu.make_async_copy(b_stage.at[slot, 0], gg_hbm.at[:, columns(c)], od.at[slot, 0]),
                pltpu.make_async_copy(b_stage.at[slot, 1], gu_hbm.at[:, columns(c)], od.at[slot, 1]),
            )
        return (pltpu.make_async_copy(b_stage.at[slot, 2], gd_hbm.at[columns(c)], od.at[slot, 2]),)

    lanes_of = (pl.ds(0, 2), pl.ds(2, 1))

    def swap(which, c):
        slot, part = lax.rem(c, 2), lanes_of[which]
        send(t_send.at[slot, part], t_recv.at[c, part], ts.at[which, slot], tr.at[which, lax.rem(c, SLOTS)], dev("c", 0))

    def grads_e(c):
        slot = lax.rem(c, 2)
        ag_done(e_kind, c)
        dgate, dup = ag_whole(e_kind, c, 0), ag_whole(e_kind, c, 1)
        dn_acc[...] += dot_nt(dgate, wg[:, columns(c)]) + dot_nt(dup, wu[:, columns(c)])

        @pl.when(c == n_chunks - 1)
        def _():
            dn_send[...] = dn_acc[...].astype(BF16)
            for d in (1, 3, 2):
                rows_to = zpart(d, 0, rows)
                send(dn_send.at[rows_to], dn_recv.at[d - 1], z_send.at[2], z_recv.at[2, d - 1], dev("z", d))

        t_send[slot, 0] = dot_nn(nrm_t[other], dgate).astype(BF16)
        t_send[slot, 1] = dot_nn(nrm_t[other], dup).astype(BF16)
        swap(0, c)
        o_stage[slot, 0] = dot_nn(nrm_t[mine], dgate)
        o_stage[slot, 1] = dot_nn(nrm_t[mine], dup)

    def grads_a(c):
        slot = lax.rem(c, 2)
        ag_done(a_kind, c)
        act = ag_whole(a_kind, c, 0)
        t_send[slot, 2] = dot_nn(dy_t[other], act).astype(BF16)
        swap(1, c)
        o_stage[slot, 2] = dot_nn(dy_t[mine], act)

    def grads_a_finish(c):
        grads_a(c)
        pl.when(c > 0)(lambda: finish(1, c - 1))

    def finish(which, c):
        slot, part = lax.rem(c, 2), lanes_of[which]
        wait(t_recv.at[c, part], tr.at[which, lax.rem(c, SLOTS)])
        wait(t_send.at[slot, part], ts.at[which, slot])

        @pl.when(c >= 2)
        def _():
            for copy in out_copies(which, c, slot):
                copy.wait()

        for k in ((0, 1), (2,))[which]:
            total = (o_stage[slot, k] + t_recv[c, k].astype(F32)).astype(BF16)
            b_stage[slot, k] = total.T if k == 2 else total
        for copy in out_copies(which, c, slot):
            copy.start()

    def sweep(count, step):
        lax.fori_loop(0, count, lambda c, _: (step(c), 0)[1], 0)

    d_kind, g_kind = kinds
    gather_relay(dy, 0)
    norm_send()
    take_dy()
    sweep(AHEAD, d_start)
    sweep(AHEAD - 1, functools.partial(rs_relay, d_kind))
    gather_relay(nrm, 1)
    sweep(AHEAD - 2, functools.partial(rs_turn, d_kind))
    sweep(AHEAD - 3, functools.partial(rs_relay2, d_kind))
    norm_take()

    def tail_sum():
        dn = dn_acc[zrows]
        for d in (1, 3, 2):
            wait(dn_recv.at[d - 1], z_recv.at[2, d - 1])
            dn = dn + dn_recv[d - 1].astype(F32)
        xhat, _ = normalised()
        dxhat = dn * gain_selected()
        ind = mod_col[:, 0:1]
        dnx = dn * xhat
        sums = [jnp.sum(v, 0, keepdims=True) for v in (dnx * (1.0 - ind), dnx * ind, dn * (1.0 - ind), dn * ind)]
        st_src[1] = pack(jnp.sum(dxhat, -1, keepdims=True), jnp.sum(dxhat * xhat, -1, keepdims=True))
        gb_src[...] = jnp.concatenate(sums + [jnp.zeros((4, feats), F32)], axis=0)
        stat_send(1)
        for d in (1, 2, 3):
            send(gb_src, gb_recv.at[d - 1], gb_send, gb_sem, dev("z", d))
        for d in range(4):
            send(gb_src, gb_recv.at[3 + d], gb_send, gb_sem, dev("c", d))
        dn_acc[zrows] = dxhat

    def tail_last():
        mean_g, mean_gx = unpack(stat_take(1))
        xhat, inv = normalised()
        ig_ref[...] = (
            inv * (dn_acc[zrows] - mean_g / WIDTH - xhat * (mean_gx / WIDTH)) + dy[zrows].astype(F32)
        ).astype(BF16)
        wait(gb_recv, gb_sem)
        gb = gb_src[...]
        for d in range(7):
            gb = gb + gb_recv[d]
        gain_out[...] = gb[0:2]
        bias_out[...] = gb[2:4]
        wait(gb_recv, gb_send)

    def tick(i, _):
        def at(off, step, *kind):
            c = i - off
            pl.when(jnp.logical_and(c >= 0, c < n_chunks))(lambda: step(*kind, c))

        def late(off, step, *kind):
            c = i - off - LAG
            count = jnp.where(i - off == n_chunks, LAG, jnp.where(i - off > n_chunks, 0, jnp.where(c >= 0, 1, 0)))
            lax.fori_loop(c, c + count, lambda k, _: (step(*kind, k), 0)[1], 0)

        at(0, g_start)
        at(-AHEAD, d_start)
        at(1, rs_relay, g_kind)
        at(1 - AHEAD, rs_relay, d_kind)
        at(2, rs_turn, g_kind)
        at(2 - AHEAD, rs_turn, d_kind)
        at(3, rs_relay2, g_kind)
        at(3 - AHEAD, rs_relay2, d_kind)
        at(4, rs_settle, g_kind)
        at(4 - AHEAD, rs_settle, d_kind)
        at(4, point)
        at(4, ag_start, e_kind)
        at(4, ag_start, a_kind)
        at(5, ag_relay, e_kind)
        at(5, ag_relay, a_kind)
        at(6, ag_turn, e_kind)
        at(7, ag_relay2, e_kind)
        at(8, grads_e)
        at(9, finish, 0)
        late(6, ag_turn, a_kind)
        late(7, ag_relay2, a_kind)
        late(8, grads_a_finish)
        pl.when(i == 7)(turn_normed)
        pl.when(i == 9)(turn_dy)
        return 0

    lax.fori_loop(0, n_chunks + 8, tick, 0)

    def rest(first_chunk, last_chunk):
        lax.fori_loop(first_chunk, last_chunk, lambda c, _: (grads_a_finish(c), 0)[1], 0)

    finish(0, n_chunks - 1)
    rest(n_chunks - LAG, n_chunks - AFTER)
    tail_sum()
    rest(n_chunks - AFTER, n_chunks)
    finish(1, n_chunks - 1)
    tail_last()

    for slot in (0, 1):
        for which in (0, 1):
            for copy in out_copies(which, 0, slot):
                copy.wait()
    wait(dy.at[pl.ds(0, 3 * rows)], z_send.at[0])
    wait(nrm.at[pl.ds(0, 3 * rows)], z_send.at[1])
    wait(dn_recv, z_send.at[2])
    for k, (src, dst) in enumerate(w_pairs):
        wait(dst, w_send.at[k])


def write_kernel(*refs):
    for src, dst in zip(refs[:6], refs[6:]):
        dst[...] = src[...].astype(dst.dtype)


def per_device(
    inputs, cotangent, modality, modality_norm_gain, modality_norm_bias, w_gate, w_up, w_down
):
    rows, feats = inputs.shape
    half = feats // 2
    tokens = rows * RING
    hidden = w_gate.shape[1]
    nc = hidden // CHUNK
    sub = rows // RING
    vmem = pl.BlockSpec(memory_space=pltpu.VMEM)
    anyw = pl.BlockSpec(memory_space=pl.ANY)

    def buf(*shape, kind=BF16):
        return pltpu.VMEM(shape, kind)

    def dma(*shape):
        return pltpu.SemaphoreType.DMA(shape)

    one = pltpu.SemaphoreType.DMA

    scratch = [
        buf(rows, feats), buf(tokens, kind=jnp.int32), buf(2, feats, kind=F32), buf(2, feats, kind=F32),
        buf(feats, hidden), buf(feats, hidden), buf(2, hidden, half),
        buf(tokens, feats), buf(feats, tokens), buf(tokens, feats), buf(feats, tokens),
        buf(tokens, feats, kind=F32), buf(tokens, feats), buf(3, rows, feats),
        buf(nc, 2, 4, 4, sub, LANES), buf(nc, 2, 4, 4, 2 * sub, LANES),
        buf(nc, 2, 4, sub, LANES), buf(nc, 2, 4, 2 * sub, LANES),
        buf(nc, 2, 2, 4, sub, LANES), buf(nc, 2, 2, 4, 2 * sub, LANES),
        buf(nc, 2, sub, LANES), buf(nc, 2, 2 * sub, LANES),
        buf(nc, 2, 2, sub, LANES), buf(nc, 2, 2, 2 * sub, LANES),
        buf(nc, 2, 4, 4, 2 * sub, LANES), buf(nc, 2, 4, 4, sub, LANES),
        buf(2, 3, CHUNK, CHUNK), buf(nc, 3, CHUNK, CHUNK), buf(2, 3, CHUNK, CHUNK, kind=F32), buf(2, 3, CHUNK, CHUNK),
        buf(2, 8, LANES, kind=F32), buf(2, 15, 8, LANES, kind=F32), buf(8, LANES, kind=F32),
        buf(8, feats, kind=F32), buf(7, 8, feats, kind=F32),
        buf(tokens, LANES, kind=F32), buf(rows, LANES, kind=F32),
        dma(5), dma(3), dma(3), dma(3), dma(3), dma(3, 3), dma(2), dma(2), one, one,
        dma(2, SLOTS), dma(2, SLOTS), dma(2, SLOTS, 2), dma(2, SLOTS, 2),
        dma(SLOTS + nc), dma(SLOTS + nc), dma(SLOTS + nc, 2), dma(SLOTS + nc, 2),
        dma(2, 2), dma(2, SLOTS), dma(2, 3),
    ]
    results = pl.pallas_call(
        functools.partial(block_kernel, nc),
        out_shape=(
            jax.ShapeDtypeStruct((rows, feats), BF16),
            jax.ShapeDtypeStruct((2, feats), F32),
            jax.ShapeDtypeStruct((2, feats), F32),
            jax.ShapeDtypeStruct((half, hidden), BF16),
            jax.ShapeDtypeStruct((half, hidden), BF16),
            jax.ShapeDtypeStruct((hidden, half), BF16),
        ),
        in_specs=[anyw] * 8,
        out_specs=(vmem, vmem, vmem, anyw, anyw, anyw),
        scratch_shapes=scratch,
        compiler_params=pltpu.CompilerParams(
            collective_id=0, has_side_effects=True, vmem_limit_bytes=63 * 2**20
        ),
        cost_estimate=pl.CostEstimate(
            flops=16 * tokens * feats * hidden, bytes_accessed=40 * 2**20, transcendentals=tokens * hidden // 16
        ),
        name="ffn_backward",
    )(inputs, cotangent, modality, modality_norm_gain, modality_norm_bias, w_gate, w_up, w_down)
    cols = pl.BlockSpec((half // 4, hidden), lambda i: (i, 0))
    down = pl.BlockSpec((hidden // 4, half), lambda i: (i, 0))
    small = [pl.BlockSpec((rows, feats), lambda i: (0, 0))] + [pl.BlockSpec((2, feats), lambda i: (0, 0))] * 2
    ig, gain_gradient, grad_bias, gg, gu, gd = pl.pallas_call(
        write_kernel,
        grid=(4,),
        out_shape=(
            jax.ShapeDtypeStruct((rows, feats), BF16),
            jax.ShapeDtypeStruct((2, feats), F32),
            jax.ShapeDtypeStruct((2, feats), F32),
            jax.ShapeDtypeStruct((half, hidden), F32),
            jax.ShapeDtypeStruct((half, hidden), F32),
            jax.ShapeDtypeStruct((hidden, half), F32),
        ),
        in_specs=small + [cols, cols, down],
        out_specs=small + [cols, cols, down],
        compiler_params=pltpu.CompilerParams(vmem_limit_bytes=63 * 2**20),
        name="write_results",
    )(*results)
    return (ig, gg, gu, gd, gain_gradient, grad_bias)


def solution(mesh):
    return jax.shard_map(
        per_device,
        mesh=mesh,
        in_specs=(
            P(("tok", "ffn"), "hid"),
            P(("tok", "ffn"), "hid"),
            P("tok"),
            P(None, "hid"),
            P(None, "hid"),
            P(("hid", "tok"), "ffn"),
            P(("hid", "tok"), "ffn"),
            P("ffn", ("hid", "tok")),
        ),
        out_specs=(
            P(("tok", "ffn"), "hid"),
            P(("hid", "tok"), "ffn"),
            P(("hid", "tok"), "ffn"),
            P("ffn", ("hid", "tok")),
            P(None, "hid"),
            P(None, "hid"),
        ),
        check_vma=False,
    )
```
